128 devices in a mesh: section: 4 (over y), expert: 32 (over z, x, core).
Axes of the slice: x: 4, y: 4, z: 4, core: 2. Of those that a mesh axis runs over, the one named last changes fastest.
Arguments:
- tokens: bfloat16 [4, 256, 3584], P('section', 'expert'), may hold values from -6 to 6
- norm_gain: bfloat16 [4, 3584], P('section'), may hold values from 0.5 to 1.5
- router: bfloat16 [4, 3584, 32], P('section'), may hold values from -0.09375 to 0.09375
- w_gate: bfloat16 [4, 32, 3584, 1024], P('section', 'expert'), may hold values from -0.09375 to 0.09375
- w_up: bfloat16 [4, 32, 3584, 1024], P('section', 'expert'), may hold values from -0.09375 to 0.09375
- w_down: bfloat16 [4, 32, 1024, 3584], P('section', 'expert'), may hold values from -0.1875 to 0.1875
- expert_ids: int32 [4, 4, 256, 8], P('section', None, 'expert'), may hold values from 0 to 31, all different within a row
Outputs:
- mixed: bfloat16 [4, 256, 3584], P('section', 'expert')
The draws below stay inside these ranges and needn't reach their ends.
Inputs may be any that keep to these rules, and one draw needn't show every extreme that they name: `expert_ids`: each row names 8 different experts.
All inputs are finite; a program needn't handle non-finite values.
Results may differ from the reference program's by a relative error of at most 0.022.
Values may be sent and summed in bfloat16 or wider, within the bound.
A program may use at most 128 MiB of HBM per device.

```python
import jax
import jax.numpy as jnp
from jax import lax

D = 3584
FF = 1024
TOPK = 8
TOK_DEV = 8
EXPERTS = 32
LAYERS = 4
MICRO = 4
TOKENS = 256
CAP = 2
N_EXPERT = 32


def shard_levels(rng, shape, cuts, smallest, high):
    factor_of, own = 1.0, jax.random.fold_in(rng, 6)
    for dim, blocks in cuts:
        heights = jnp.exp(jax.random.uniform(jax.random.fold_in(own, dim), (blocks,), jnp.float32, smallest / len(cuts), high / len(cuts)))
        factor_of = factor_of * jnp.repeat(heights, shape[dim] // blocks).reshape([-1 if axis == dim else 1 for axis in range(len(shape))])
    return factor_of


def picks_of(rng, rows, number_of, top, lift):
    order = jax.random.permutation(jax.random.fold_in(rng, 1), number_of)
    pull = order
    for power in range(3):
        pull = pull * pull // number_of
    pull = pull * lift // number_of
    tickets = jax.random.randint(jax.random.fold_in(rng, 2), (rows, number_of), 0, 4096) + pull
    holders = jax.random.permutation(jax.random.fold_in(rng, 3), rows)[jnp.arange(number_of) % rows]
    tickets = jnp.where(jnp.arange(rows)[:, None] == holders[None, :], 1 << 14, tickets)
    priority = tickets * number_of + jnp.arange(number_of)
    return lax.top_k(priority.astype(jnp.int32), top)[1].astype(jnp.int32)


def centred(rng, extent, width, most, split=(), kind=jnp.bfloat16):
    loudness = shard_levels(rng, extent, split, -0.22, 0.18) if split else 1.0
    values = jax.random.normal(rng, extent, jnp.float32) * width * loudness
    return jnp.minimum(jnp.maximum(values, -most), most).astype(kind)


def setup_inputs(seed: int = 0) -> dict:
    splits = jax.random.split(jax.random.key(seed), 8)
    tokens = centred(splits[0], (MICRO, TOKENS, D), 1.0, 6.0, ((0, 4), (1, 32)))
    norm_gain = jnp.clip(1.0 + 0.1 * jax.random.normal(splits[1], (LAYERS, D), jnp.float32), 0.5, 1.5).astype(jnp.bfloat16)
    router = centred(splits[2], (LAYERS, D, EXPERTS), D ** -0.5, 0.09375, ((0, 4),))
    w_gate = centred(splits[3], (LAYERS, EXPERTS, D, FF), D ** -0.5, 0.09375, ((0, 4), (1, 32)))
    w_up = centred(splits[4], (LAYERS, EXPERTS, D, FF), D ** -0.5, 0.09375, ((0, 4), (1, 32)))
    w_down = centred(splits[5], (LAYERS, EXPERTS, FF, D), FF ** -0.5, 0.1875, ((0, 4), (1, 32)))
    expert_ids = picks_of(splits[6], LAYERS * MICRO * TOKENS, EXPERTS, TOPK, 4096).reshape((LAYERS, MICRO, TOKENS, TOPK))
    return {"tokens": tokens, "norm_gain": norm_gain, "router": router, "w_gate": w_gate, "w_up": w_up, "w_down": w_down, "expert_ids": expert_ids}


epsilon = 1e-06
routed_scale = 2.5

def normalize(hidden_rows, gain_row):
    values = hidden_rows.astype(jnp.float32)
    inverse_rms = lax.rsqrt(lax.optimization_barrier(jnp.mean(values * values, axis=-1, keepdims=True)) + epsilon)
    return (values * inverse_rms * gain_row.astype(jnp.float32)).astype(jnp.bfloat16)

def route(normed, choices, router_cols, blocks):
    expert_count = router_cols.shape[1]
    logits = jnp.dot(normed, router_cols, preferred_element_type=jnp.float32)
    scores = jax.nn.sigmoid(logits)
    onehot = choices[:, :, None] == jnp.arange(expert_count, dtype=jnp.int32)[None, None, :]
    picked = lax.optimization_barrier(jnp.sum(jnp.where(onehot, scores[:, None, :], 0.0), axis=-1))
    weights = routed_scale * picked / lax.optimization_barrier(jnp.sum(picked, axis=-1, keepdims=True))
    indicator = onehot.astype(jnp.int32).reshape(blocks, -1, expert_count)
    earlier = jnp.cumsum(indicator, axis=1) - indicator
    positions = lax.optimization_barrier(jnp.sum(earlier * indicator, axis=-1)).reshape(choices.shape)
    return (weights, positions.astype(jnp.int32))

def expert_mlp(inputs, gate_weight, up_weight, down_weight):
    gate_part = jnp.dot(inputs, gate_weight, preferred_element_type=jnp.float32)
    up_part = jnp.dot(inputs, up_weight, preferred_element_type=jnp.float32)
    hidden = (jax.nn.silu(gate_part) * up_part).astype(jnp.bfloat16)
    return jnp.dot(hidden, down_weight, preferred_element_type=jnp.float32).astype(jnp.bfloat16)

def moe_layer(hidden_rows, gain_row, router_cols, gate_all, up_all, down_all, choices):
    normed = normalize(hidden_rows, gain_row)
    weights, positions = route(normed, choices, router_cols, N_EXPERT)
    retained = positions < CAP
    source_block = (jnp.arange(TOKENS, dtype=jnp.int32) // TOK_DEV)[:, None]
    slot_keys = (choices * (N_EXPERT * CAP) + source_block * CAP + positions).astype(jnp.int32)
    total_slots = EXPERTS * N_EXPERT * CAP
    target = jnp.where(retained, slot_keys, total_slots).astype(jnp.int32)
    buffer = jnp.zeros((total_slots, D), jnp.bfloat16).at[target.reshape(-1)].set(jnp.repeat(normed, TOPK, axis=0), mode='drop')

    def serve_expert(operands):
        rows_in, gate_weight, up_weight, down_weight = operands
        return expert_mlp(rows_in, gate_weight, up_weight, down_weight)
    produced = lax.map(serve_expert, (buffer.reshape(EXPERTS, N_EXPERT * CAP, D), gate_all, up_all, down_all))
    flattened = produced.reshape(total_slots, D)
    picked = flattened[jnp.where(retained, slot_keys, 0).astype(jnp.int32)]
    factor = jnp.where(retained, weights, 0.0)
    branch = jnp.einsum('tk,tkd->td', factor, picked.astype(jnp.float32))
    return (hidden_rows.astype(jnp.float32) + branch).astype(jnp.bfloat16)

def reference(tokens, norm_gain, router, w_gate, w_up, w_down, expert_ids):
    outputs = []
    for micro_index in range(MICRO):
        hidden_rows = tokens[micro_index]
        for layer_index in range(LAYERS):
            hidden_rows = moe_layer(hidden_rows, norm_gain[layer_index], router[layer_index], w_gate[layer_index], w_up[layer_index], w_down[layer_index], expert_ids[layer_index, micro_index])
        outputs.append(hidden_rows)
    return jnp.stack(outputs)
```

```python
import functools

import jax
import jax.numpy as jnp
from jax import lax
from jax.experimental import pallas as pl
from jax.experimental.pallas import tpu as pltpu
from jax.sharding import PartitionSpec as P

MESH = pl.DeviceIdType.MESH
BF16 = jnp.bfloat16
F32 = jnp.float32

epsilon = 1e-06
routed_scale = 2.5
capacity = 2
lane = 128
slot_rows = 32
message_rows = capacity * slot_rows


def dot(a, b):
    return jnp.dot(a, b, preferred_element_type=F32)


def iota(shape, dim):
    return lax.broadcasted_iota(jnp.int32, shape, dim)


def ones_where(mask, dtype=BF16):
    return jnp.where(mask, 1.0, 0.0).astype(dtype)


def schedule(micros):
    order = [(0, 0)]
    for m in range(micros):
        if m + 1 < micros:
            order.append((0, m + 1))
        order.append((1, m))
        if m >= 1:
            order.append((2, m - 1))
    order.append((2, micros - 1))
    return order


def kernel(
    grid_z, grid_x, sections, chunks, tokens, gain, router, w_gate, w_up, w_down, ids, result,
    gate_v, up_v, down_v, hidden, finished, staged, outgoing,
    place, pick, factors, stacked, dispatched, arrived, produced, returned,
    rows_in, inner, columns, select, select_t, spread, mask_j,
    gate_sem, up_sem, down_sem, hidden_sem, hidden_send, finished_sem,
    dispatch_send, arrive_sem, produce_send, return_sem, local_sem,
):
    section = lax.axis_index("section")
    me = lax.axis_index("expert")
    experts = grid_z * grid_x * 2
    micros = sections
    rows = 8
    width = chunks * lane
    half = width // 2
    inner_width = gate_v.shape[1]
    core, x, z = lax.rem(me, 2), lax.rem(me // 2, grid_x), me // (2 * grid_x)

    def distance(step, size):
        return min(step, size - step)

    offsets = [(dz, dx, dc) for dz in range(grid_z) for dx in range(grid_x) for dc in range(2)]
    offsets.sort(key=lambda o: -(10 * (distance(o[0], grid_z) + distance(o[1], grid_x)) + o[2]))
    partners = []
    for dz, dx, dc in offsets[:-1]:
        partners.append(
            lax.rem(z + dz, grid_z) * (2 * grid_x) + lax.rem(x + dx, grid_x) * 2 + lax.rem(core + dc, 2)
        )

    copy_gate = pltpu.make_async_copy(w_gate.at[0, 0], gate_v, gate_sem)
    copy_up = pltpu.make_async_copy(w_up.at[0, 0], up_v, up_sem)
    copy_down = pltpu.make_async_copy(w_down.at[0, 0], down_v, down_sem)
    copy_gate.start()
    copy_up.start()
    copy_down.start()

    barrier = pltpu.get_barrier_semaphore()
    for partner in partners:
        pl.semaphore_signal(barrier, inc=1, device_id={"expert": partner}, device_id_type=MESH)
    for step in range(1, sections):
        pl.semaphore_signal(
            barrier, inc=1, device_id={"section": lax.rem(section + step, sections)}, device_id_type=MESH
        )

    used = chunks * rows
    shape = (used, 4 * message_rows)
    r, c = iota(shape, 0), iota(shape, 1)
    select[...] = ones_where(c == ((r % 8) // 2) * message_rows + (r % 2) * slot_rows + r // 8)
    shape = (4 * message_rows, 256)
    r, c = iota(shape, 0), iota(shape, 1)
    select_t[...] = ones_where(
        (c < used) & (r == ((c % 8) // 2) * message_rows + (c % 2) * slot_rows + c // 8)
    )
    shape = (experts, experts * message_rows)
    r, c = iota(shape, 0), iota(shape, 1)
    for p in range(capacity):
        spread[p] = ones_where((c // message_rows == r) & ((c % message_rows) // slot_rows == p))
    shape = (chunks * 16, lane)
    r, c = iota(shape, 0), iota(shape, 1)
    mask_j[...] = ones_where(c % slot_rows == r // 16)
    for m in range(micros):
        stacked[m, used:, :] = jnp.zeros((256 - used, lane), BF16)
    for g in range(experts // 4):
        columns[g, used:, :] = jnp.zeros((256 - used, lane), BF16)

    shape = (slot_rows, 256)
    r, c = iota(shape, 0), iota(shape, 1)
    diagonal = jnp.where((c // rows == r) & (r < chunks), 1.0, 0.0).astype(F32)
    repeat = jnp.where(iota((rows, 256), 1) % rows == iota((rows, 256), 0), 1.0, 0.0).astype(F32)
    token_of = iota((rows, experts), 0)
    expert_of = iota((rows, experts), 1)

    def plan(m, _):
        choices = ids[0, m]
        hit = jnp.zeros((rows, experts), F32)
        for k in range(choices.shape[1]):
            hit = hit + jnp.where(choices[:, k : k + 1] == expert_of, 1.0, 0.0)
        before = jnp.zeros((rows, experts), F32)
        for t in range(rows - 1):
            before = before + jnp.where(token_of > t, 1.0, 0.0) * hit[t : t + 1, :]
        for p in range(capacity):
            taken = jnp.where(before == float(p), hit, 0.0)
            pick[m, p] = taken
            lanes = lax.dot_general(
                taken, repeat, (((0,), (0,)), ((), ())), preferred_element_type=F32
            )
            for e in range(experts):
                place[m, e * message_rows + p * slot_rows : e * message_rows + (p + 1) * slot_rows, :] = (
                    diagonal * lanes[e : e + 1, :]
                ).astype(BF16)
        return 0

    lax.fori_loop(0, micros, plan, 0)

    held = tokens[0].astype(F32)
    staged[...] = jnp.concatenate([held[:, :half], held[:, half:]], axis=0).astype(BF16)
    pl.semaphore_wait(barrier, len(partners) + sections - 1)

    first_copy = pltpu.make_async_remote_copy(
        src_ref=staged, dst_ref=hidden.at[section], send_sem=local_sem, recv_sem=hidden_sem.at[section],
        device_id={"section": 0}, device_id_type=MESH,
    )

    @pl.when(section == 0)
    def _():
        hidden[0] = staged[...]

    @pl.when(section != 0)
    def _():
        first_copy.start()

    def load_hidden(m):
        packed = hidden[m].astype(F32)
        return jnp.concatenate([packed[:rows], packed[rows:]], axis=1)

    def dispatch(m):
        @pl.when((section != 0) | (m != 0))
        def _():
            pltpu.make_async_copy(hidden.at[m], hidden.at[m], hidden_sem.at[m]).wait()

        values = load_hidden(m)
        inverse_rms = lax.rsqrt(jnp.mean(values * values, axis=-1, keepdims=True) + epsilon)
        normed = values * inverse_rms * gain[...].astype(F32)
        stacked[m, :used, :] = jnp.concatenate(
            [normed[:, j * lane : (j + 1) * lane] for j in range(chunks)], axis=0
        ).astype(BF16)
        dispatched[m] = dot(place[m], stacked[m]).astype(BF16)
        here = pl.multiple_of(me * message_rows, message_rows)
        for partner in partners:
            there = pl.multiple_of(partner * message_rows, message_rows)
            pltpu.make_async_remote_copy(
                src_ref=dispatched.at[m, pl.ds(there, message_rows)],
                dst_ref=arrived.at[m, pl.ds(here, message_rows)],
                send_sem=dispatch_send.at[m], recv_sem=arrive_sem.at[m],
                device_id={"expert": partner}, device_id_type=MESH,
            ).start()
        pltpu.make_async_copy(
            dispatched.at[m, pl.ds(here, message_rows)],
            arrived.at[m, pl.ds(here, message_rows)],
            arrive_sem.at[m],
        ).start()

        twice = jnp.concatenate([normed, normed], axis=0).astype(BF16)
        scores = jax.nn.sigmoid(dot(twice, router[0])[:rows])
        kept = [pick[m, p] for p in range(capacity)]
        chosen = jnp.zeros((rows, experts), F32)
        for k in range(ids.shape[3]):
            chosen = chosen + jnp.where(ids[0, m][:, k : k + 1] == expert_of, scores, 0.0)
        weights = routed_scale * scores / jnp.sum(chosen, axis=-1, keepdims=True)
        wide = None
        for p in range(capacity):
            factor = weights * kept[p]
            high = factor.astype(BF16).astype(F32)
            both = jnp.concatenate([high, factor - high], axis=0).astype(BF16)
            part = dot(both, spread[p])
            wide = part if wide is None else wide + part
        wide = wide.astype(BF16)
        for j in range(chunks):
            mask = mask_j[j * 16 : (j + 1) * 16, :]
            factors[m, j * 16 : (j + 1) * 16, :] = wide * jnp.concatenate(
                [mask] * (experts * message_rows // lane), axis=1
            )

    def run_experts(m):
        pltpu.make_async_copy(arrived.at[m], arrived.at[m], arrive_sem.at[m]).wait()
        group = 4 * message_rows
        for pair in range(experts // 8):
            first = arrived[m, (2 * pair) * group : (2 * pair + 1) * group, :]
            second = arrived[m, (2 * pair + 1) * group : (2 * pair + 2) * group, :]
            sorted_rows = dot(select[...], jnp.concatenate([first, second], axis=1))
            for j in range(chunks):
                tile = sorted_rows[j * 8 : (j + 1) * 8, :]
                rows_in[pair * 16 : (pair + 1) * 16, j * lane : (j + 1) * lane] = jnp.concatenate(
                    [tile[:, :lane], tile[:, lane:]], axis=0
                ).astype(BF16)

        @pl.when(m == 0)
        def _():
            copy_gate.wait()
            copy_up.wait()

        for n in range(inner_width // 256):
            cols = slice(n * 256, (n + 1) * 256)
            gate_part = dot(rows_in[...], gate_v[:, cols])
            up_part = dot(rows_in[...], up_v[:, cols])
            inner[:, cols] = (gate_part / (1.0 + jnp.exp(-gate_part)) * up_part).astype(BF16)

        @pl.when(m == 0)
        def _():
            copy_down.wait()

        step = 4
        for n in range(chunks // step):
            out = dot(inner[...], down_v[:, n * step * lane : (n + 1) * step * lane])
            for g in range(experts // 4):
                columns[g, n * step * 8 : (n + 1) * step * 8, :] = jnp.concatenate(
                    [out[g * 8 : (g + 1) * 8, j * lane : (j + 1) * lane] for j in range(step)], axis=0
                ).astype(BF16)
        for pair in range(experts // 8):
            both = jnp.concatenate([columns[2 * pair], columns[2 * pair + 1]], axis=1)
            back = dot(select_t[...], both).astype(BF16)
            produced[m, (2 * pair) * group : (2 * pair + 1) * group, :] = back[:, :lane]
            produced[m, (2 * pair + 1) * group : (2 * pair + 2) * group, :] = back[:, lane:]
        here = pl.multiple_of(me * message_rows, message_rows)
        for partner in partners:
            there = pl.multiple_of(partner * message_rows, message_rows)
            pltpu.make_async_remote_copy(
                src_ref=produced.at[m, pl.ds(there, message_rows)],
                dst_ref=returned.at[m, pl.ds(here, message_rows)],
                send_sem=produce_send.at[m], recv_sem=return_sem.at[m],
                device_id={"expert": partner}, device_id_type=MESH,
            ).start()
        pltpu.make_async_copy(
            produced.at[m, pl.ds(here, message_rows)],
            returned.at[m, pl.ds(here, message_rows)],
            return_sem.at[m],
        ).start()

    def combine(m):
        pltpu.make_async_copy(returned.at[m], returned.at[m], return_sem.at[m]).wait()
        branch = dot(factors[m], returned[m])
        values = load_hidden(m)
        fresh = []
        for j in range(chunks):
            part = branch[j * 16 : j * 16 + 8, :] + branch[j * 16 + 8 : j * 16 + 16, :]
            fresh.append(values[:, j * lane : (j + 1) * lane] + part)
        split = chunks // 2
        outgoing[m] = jnp.concatenate(
            [jnp.concatenate(fresh[:split], axis=1), jnp.concatenate(fresh[split:], axis=1)], axis=0
        ).astype(BF16)

        @pl.when(section < sections - 1)
        def _():
            pltpu.make_async_remote_copy(
                src_ref=outgoing.at[m], dst_ref=hidden.at[m],
                send_sem=hidden_send.at[m], recv_sem=hidden_sem.at[m],
                device_id={"section": lax.rem(section + 1, sections)}, device_id_type=MESH,
            ).start()

        @pl.when((section == sections - 1) & (m < micros - 1))
        def _():
            pltpu.make_async_remote_copy(
                src_ref=outgoing.at[m], dst_ref=finished,
                send_sem=hidden_send.at[m], recv_sem=finished_sem,
                device_id={"section": lax.rem(m, sections)}, device_id_type=MESH,
            ).start()

        @pl.when((section == sections - 1) & (m == micros - 1))
        def _():
            finished[...] = outgoing[m]

    order = schedule(micros)

    def stage(i, _):
        kind, m = jnp.int32(order[0][0]), jnp.int32(order[0][1])
        for index, (k, micro) in enumerate(order):
            kind = jnp.where(i == index, k, kind)
            m = jnp.where(i == index, micro, m)

        @pl.when(kind == 0)
        def _():
            dispatch(m)

        @pl.when(kind == 1)
        def _():
            run_experts(m)

        @pl.when(kind == 2)
        def _():
            combine(m)

        return 0

    lax.fori_loop(0, len(order), stage, 0)

    @pl.when(section < sections - 1)
    def _():
        pltpu.make_async_copy(finished, finished, finished_sem).wait()

    packed = finished[...].astype(F32)
    result[0] = jnp.concatenate([packed[:rows], packed[rows:]], axis=1).astype(BF16)

    @pl.when(section != 0)
    def _():
        first_copy.wait_send()

    def drain(m, _):
        sent = len(partners) * message_rows
        for source, semaphore in ((dispatched, dispatch_send), (produced, produce_send)):
            view = source.at[m, pl.ds(0, sent)]
            pltpu.make_async_copy(view, view, semaphore.at[m]).wait()

        @pl.when((section < sections - 1) | (m < micros - 1))
        def _():
            pltpu.make_async_copy(outgoing.at[m], outgoing.at[m], hidden_send.at[m]).wait()

        return 0

    lax.fori_loop(0, micros, drain, 0)


def solution(mesh):
    sections = mesh.shape["section"]
    experts = mesh.shape["expert"]
    grid_z = grid_x = int(round((experts // 2) ** 0.5))

    def per_device(tokens, norm_gain, router, w_gate, w_up, w_down, expert_ids):
        rows, width = tokens.shape[1:]
        inner_width = w_gate.shape[3]
        chunks = width // lane
        micros = expert_ids.shape[1]
        used = chunks * rows
        slots = experts * capacity
        messages = experts * message_rows
        vmem = pl.BlockSpec(memory_space=pltpu.VMEM)
        anywhere = pl.BlockSpec(memory_space=pl.ANY)
        dma = pltpu.SemaphoreType.DMA
        packed = (2 * rows, width // 2)
        return pl.pallas_call(
            functools.partial(kernel, grid_z, grid_x, sections, chunks),
            out_shape=jax.ShapeDtypeStruct(tokens.shape, BF16),
            in_specs=[vmem, vmem, vmem, anywhere, anywhere, anywhere, vmem],
            out_specs=vmem,
            scratch_shapes=[
                pltpu.VMEM((width, inner_width), BF16),
                pltpu.VMEM((width, inner_width), BF16),
                pltpu.VMEM((inner_width, width), BF16),
                pltpu.VMEM((micros,) + packed, BF16),
                pltpu.VMEM(packed, BF16),
                pltpu.VMEM(packed, BF16),
                pltpu.VMEM((micros,) + packed, BF16),
                pltpu.VMEM((micros, messages, 256), BF16),
                pltpu.VMEM((micros, capacity, rows, experts), F32),
                pltpu.VMEM((micros, chunks * 16, messages), BF16),
                pltpu.VMEM((micros, 256, lane), BF16),
                pltpu.VMEM((micros, messages, lane), BF16),
                pltpu.VMEM((micros, messages, lane), BF16),
                pltpu.VMEM((micros, messages, lane), BF16),
                pltpu.VMEM((micros, messages, lane), BF16),
                pltpu.VMEM((slots, width), BF16),
                pltpu.VMEM((slots, inner_width), BF16),
                pltpu.VMEM((experts // 4, 256, lane), BF16),
                pltpu.VMEM((used, 4 * message_rows), BF16),
                pltpu.VMEM((4 * message_rows, 256), BF16),
                pltpu.VMEM((capacity, experts, messages), BF16),
                pltpu.VMEM((chunks * 16, lane), BF16),
                dma, dma, dma,
                dma((micros,)), dma((micros,)), dma,
                dma((micros,)), dma((micros,)), dma((micros,)), dma((micros,)), dma,
            ],
            compiler_params=pltpu.CompilerParams(
                collective_id=0, has_side_effects=True, vmem_limit_bytes=58 * 2**20
            ),
            name="expert_layers",
        )(tokens, norm_gain, router, w_gate, w_up, w_down, expert_ids)

    placed = (
        P("section", "expert", None),
        P("section", None),
        P("section", None, None),
        P("section", "expert", None, None),
        P("section", "expert", None, None),
        P("section", "expert", None, None),
        P("section", None, "expert", None),
    )
    return jax.shard_map(
        per_device,
        mesh=mesh,
        in_specs=placed,
        out_specs=P("section", "expert", None),
        check_vma=False,
    )
```

```python
import functools

import jax
import jax.numpy as jnp
from jax import lax
from jax.experimental import pallas as pl
from jax.experimental.pallas import tpu as pltpu
from jax.sharding import PartitionSpec as P

MESH = pl.DeviceIdType.MESH
BF16 = jnp.bfloat16
F32 = jnp.float32

epsilon = 1e-06
routed_scale = 2.5
capacity = 2
lane = 128
message_rows = 64


def dot(a, b):
    return jnp.dot(a, b, preferred_element_type=F32)


def iota(shape, dim):
    return lax.broadcasted_iota(jnp.int32, shape, dim)


def ones_where(mask, dtype=BF16):
    return jnp.where(mask, 1.0, 0.0).astype(dtype)


def schedule(micros):
    order = []
    for m in range(0, micros, 2):
        if m:
            order += [(2, m - 2), (0, m), (2, m - 1), (0, m + 1), (1, m), (1, m + 1)]
        else:
            order += [(0, 0), (0, 1), (1, 0), (1, 1)]
    return order + [(2, micros - 2), (2, micros - 1)]


def kernel(
    grid_z, grid_x, sections, chunks, tokens, gain, router, w_gate, w_up, w_down, ids, result,
    gate_v, up_v, down_v, hidden, finished, staged, outgoing,
    place, pick, factors, stacked, dispatched, arrived, produced, returned,
    rows_in, inner, columns, select, select_t, spread, mask_j,
    gate_sem, up_sem, down_sem, hidden_sem, hidden_send, finished_sem,
    dispatch_send, arrive_sem, produce_send, return_sem, local_sem,
):
    section = lax.axis_index("section")
    me = lax.axis_index("expert")
    experts = grid_z * grid_x * 2
    micros = sections
    rows = 8
    width = chunks * lane
    half = width // 2
    inner_width = gate_v.shape[1]
    core, x, z = lax.rem(me, 2), lax.rem(me // 2, grid_x), me // (2 * grid_x)

    def distance(step, size):
        return min(step, size - step)

    offsets = [(dz, dx, dc) for dz in range(grid_z) for dx in range(grid_x) for dc in range(2)]
    offsets.sort(key=lambda o: -(10 * (distance(o[0], grid_z) + distance(o[1], grid_x)) + o[2]))
    partners = []
    for dz, dx, dc in offsets[:-1]:
        partners.append(
            lax.rem(z + dz, grid_z) * (2 * grid_x) + lax.rem(x + dx, grid_x) * 2 + lax.rem(core + dc, 2)
        )

    copy_gate = pltpu.make_async_copy(w_gate.at[0, 0], gate_v, gate_sem)
    copy_up = pltpu.make_async_copy(w_up.at[0, 0], up_v, up_sem)
    copy_down = pltpu.make_async_copy(w_down.at[0, 0], down_v, down_sem)
    copy_gate.start()
    copy_up.start()
    copy_down.start()

    for room in (arrived, returned):
        for m in range(micros):
            room[m, :, message_rows - 16 :, :] = jnp.zeros((experts, 16, lane), BF16)

    barrier = pltpu.get_barrier_semaphore()
    for partner in partners:
        pl.semaphore_signal(barrier, inc=1, device_id={"expert": partner}, device_id_type=MESH)
    for step in range(1, sections):
        pl.semaphore_signal(
            barrier, inc=1, device_id={"section": lax.rem(section + step, sections)}, device_id_type=MESH
        )

    used = chunks * rows
    sent = chunks * capacity
    for m in range(micros):
        stacked[m, used:, :] = jnp.zeros((256 - used, lane), BF16)

    shape = (message_rows, 256)
    r, c = iota(shape, 0), iota(shape, 1)
    diagonal = [
        jnp.where((c // rows == r // capacity) & (r % capacity == p) & (r < sent), 1.0, 0.0).astype(F32)
        for p in range(capacity)
    ]
    repeat = jnp.where(iota((rows, 256), 1) % rows == iota((rows, 256), 0), 1.0, 0.0).astype(F32)
    token_of = iota((rows, experts), 0)
    expert_of = iota((rows, experts), 1)

    def plan(m, _=0):
        choices = ids[0, m]
        hit = jnp.zeros((rows, experts), F32)
        for k in range(choices.shape[1]):
            hit = hit + jnp.where(choices[:, k : k + 1] == expert_of, 1.0, 0.0)
        before = jnp.zeros((rows, experts), F32)
        for t in range(rows - 1):
            before = before + jnp.where(token_of > t, 1.0, 0.0) * hit[t : t + 1, :]
        lanes = []
        for p in range(capacity):
            taken = jnp.where(before == float(p), hit, 0.0)
            pick[m, p] = taken
            lanes.append(
                lax.dot_general(taken, repeat, (((0,), (0,)), ((), ())), preferred_element_type=F32)
            )
        for e in range(experts):
            block = diagonal[0] * lanes[0][e : e + 1, :] + diagonal[1] * lanes[1][e : e + 1, :]
            place[m, e * message_rows : (e + 1) * message_rows, :] = block.astype(BF16)
        return 0

    def load_hidden(m):
        packed = hidden[m].astype(F32)
        return jnp.concatenate([packed[:rows], packed[rows:]], axis=1)

    def normalize(m):
        values = load_hidden(m)
        inverse_rms = lax.rsqrt(jnp.mean(values * values, axis=-1, keepdims=True) + epsilon)
        return values * inverse_rms * gain[...].astype(F32)

    def fill_slots(m):
        normed = normalize(m)
        stacked[m, :used, :] = jnp.concatenate(
            [normed[:, j * lane : (j + 1) * lane] for j in range(chunks)], axis=0
        ).astype(BF16)
        dispatched[m] = dot(place[m], stacked[m]).astype(BF16).reshape(experts, message_rows, lane)

    def send_slots(m):
        for partner in partners:
            pltpu.make_async_remote_copy(
                src_ref=dispatched.at[m, partner, pl.ds(0, sent)],
                dst_ref=arrived.at[m, me, pl.ds(0, sent)],
                send_sem=dispatch_send.at[m], recv_sem=arrive_sem.at[m],
                device_id={"expert": partner}, device_id_type=MESH,
            ).start()
        pltpu.make_async_copy(
            dispatched.at[m, me, pl.ds(0, sent)],
            arrived.at[m, me, pl.ds(0, sent)],
            arrive_sem.at[m],
        ).start()

    def spread_factors(m):
        normed = normalize(m)
        twice = jnp.concatenate([normed, normed], axis=0).astype(BF16)
        logits = lax.dot_general(
            twice, router[0], (((1,), (1,)), ((), ())), preferred_element_type=F32
        )
        scores = jax.nn.sigmoid(logits[:rows])
        kept = [pick[m, p] for p in range(capacity)]
        chosen = jnp.zeros((rows, experts), F32)
        for k in range(ids.shape[3]):
            chosen = chosen + jnp.where(ids[0, m][:, k : k + 1] == expert_of, scores, 0.0)
        weights = routed_scale * scores / jnp.sum(chosen, axis=-1, keepdims=True)
        wide = None
        for p in range(capacity):
            factor = weights * kept[p]
            high = factor.astype(BF16).astype(F32)
            both = jnp.concatenate([high, factor - high], axis=0).astype(BF16)
            part = dot(both, spread[p])
            wide = part if wide is None else wide + part
        wide = wide.astype(BF16)
        for j in range(chunks):
            mask = mask_j[j * 16 : (j + 1) * 16, :]
            factors[m, j * 16 : (j + 1) * 16, :] = wide * jnp.concatenate(
                [mask] * (experts * message_rows // lane), axis=1
            )

    def dispatch(m):
        @pl.when((section != 0) | (m != 0))
        def _():
            pltpu.make_async_copy(hidden.at[m], hidden.at[m], hidden_sem.at[m]).wait()
            fill_slots(m)
            send_slots(m)

        spread_factors(m)

    def run_experts(m):
        view = arrived.at[m, :, pl.ds(0, sent)]
        pltpu.make_async_copy(view, view, arrive_sem.at[m]).wait()
        group = 4 * message_rows
        for pair in range(experts // 8):
            first = arrived[m, 8 * pair : 8 * pair + 4].reshape(group, lane)
            second = arrived[m, 8 * pair + 4 : 8 * pair + 8].reshape(group, lane)
            sorted_rows = dot(select[...], jnp.concatenate([first, second], axis=1))
            for j in range(chunks):
                tile = sorted_rows[j * 8 : (j + 1) * 8, :]
                rows_in[pair * 16 : (pair + 1) * 16, j * lane : (j + 1) * lane] = jnp.concatenate(
                    [tile[:, :lane], tile[:, lane:]], axis=0
                ).astype(BF16)

        @pl.when(m == 0)
        def _():
            copy_gate.wait()
            copy_up.wait()

        for n in range(inner_width // 256):
            cols = slice(n * 256, (n + 1) * 256)
            gate_part = dot(rows_in[...], gate_v[:, cols])
            up_part = dot(rows_in[...], up_v[:, cols])
            inner[:, cols] = (gate_part / (1.0 + jnp.exp(-gate_part)) * up_part).astype(BF16)

        @pl.when(m == 0)
        def _():
            copy_down.wait()

        step = 4
        for n in range(chunks // step):
            out = dot(inner[...], down_v[:, n * step * lane : (n + 1) * step * lane])
            for g in range(experts // 4):
                columns[g, n * step * 8 : (n + 1) * step * 8, :] = jnp.concatenate(
                    [out[g * 8 : (g + 1) * 8, j * lane : (j + 1) * lane] for j in range(step)], axis=0
                ).astype(BF16)
        for pair in range(experts // 8):
            both = jnp.concatenate([columns[2 * pair], columns[2 * pair + 1]], axis=1)
            back = dot(select_t[...], both).astype(BF16)
            produced[m, 8 * pair : 8 * pair + 4] = back[:, :lane].reshape(4, message_rows, lane)
            produced[m, 8 * pair + 4 : 8 * pair + 8] = back[:, lane:].reshape(4, message_rows, lane)
        for partner in partners:
            pltpu.make_async_remote_copy(
                src_ref=produced.at[m, partner, pl.ds(0, sent)],
                dst_ref=returned.at[m, me, pl.ds(0, sent)],
                send_sem=produce_send.at[m], recv_sem=return_sem.at[m],
                device_id={"expert": partner}, device_id_type=MESH,
            ).start()
        pltpu.make_async_copy(
            produced.at[m, me, pl.ds(0, sent)],
            returned.at[m, me, pl.ds(0, sent)],
            return_sem.at[m],
        ).start()

    def combine(m):
        view = returned.at[m, :, pl.ds(0, sent)]
        pltpu.make_async_copy(view, view, return_sem.at[m]).wait()
        branch = dot(factors[m], returned[m].reshape(experts * message_rows, lane))
        values = load_hidden(m)
        fresh = []
        for j in range(chunks):
            part = branch[j * 16 : j * 16 + 8, :] + branch[j * 16 + 8 : j * 16 + 16, :]
            fresh.append(values[:, j * lane : (j + 1) * lane] + part)
        split = chunks // 2
        outgoing[m] = jnp.concatenate(
            [jnp.concatenate(fresh[:split], axis=1), jnp.concatenate(fresh[split:], axis=1)], axis=0
        ).astype(BF16)

        @pl.when(section < sections - 1)
        def _():
            pltpu.make_async_remote_copy(
                src_ref=outgoing.at[m], dst_ref=hidden.at[m],
                send_sem=hidden_send.at[m], recv_sem=hidden_sem.at[m],
                device_id={"section": lax.rem(section + 1, sections)}, device_id_type=MESH,
            ).start()

        @pl.when((section == sections - 1) & (m < micros - 1))
        def _():
            pltpu.make_async_remote_copy(
                src_ref=outgoing.at[m], dst_ref=finished,
                send_sem=hidden_send.at[m], recv_sem=finished_sem,
                device_id={"section": lax.rem(m, sections)}, device_id_type=MESH,
            ).start()

        @pl.when((section == sections - 1) & (m == micros - 1))
        def _():
            finished[...] = outgoing[m]

    held = tokens[0].astype(F32)
    staged[...] = jnp.concatenate([held[:, :half], held[:, half:]], axis=0).astype(BF16)
    plan(0)

    @pl.when(section == 0)
    def _():
        hidden[0] = staged[...]
        fill_slots(0)

    pl.semaphore_wait(barrier, len(partners) + sections - 1)

    first_copy = pltpu.make_async_remote_copy(
        src_ref=staged, dst_ref=hidden.at[section], send_sem=local_sem, recv_sem=hidden_sem.at[section],
        device_id={"section": 0}, device_id_type=MESH,
    )

    @pl.when(section == 0)
    def _():
        send_slots(0)

    @pl.when(section != 0)
    def _():
        first_copy.start()

    shape = (used, 4 * message_rows)
    r, c = iota(shape, 0), iota(shape, 1)
    select[...] = ones_where(c == ((r % 8) // 2) * message_rows + (r // 8) * 2 + r % 2)
    shape = (4 * message_rows, 256)
    r, c = iota(shape, 0), iota(shape, 1)
    select_t[...] = ones_where(
        (c < used) & (r == ((c % 8) // 2) * message_rows + (c // 8) * 2 + c % 2)
    )
    shape = (experts, experts * message_rows)
    r, c = iota(shape, 0), iota(shape, 1)
    for p in range(capacity):
        spread[p] = ones_where((c // message_rows == r) & (c % capacity == p))
    shape = (chunks * 16, lane)
    r, c = iota(shape, 0), iota(shape, 1)
    mask_j[...] = ones_where((c % message_rows) // capacity == r // 16)
    for g in range(experts // 4):
        columns[g, used:, :] = jnp.zeros((256 - used, lane), BF16)

    lax.fori_loop(1, micros, plan, 0)

    order = schedule(micros)

    def stage(i, _):
        kind, m = jnp.int32(order[0][0]), jnp.int32(order[0][1])
        for index, (k, micro) in enumerate(order):
            kind = jnp.where(i == index, k, kind)
            m = jnp.where(i == index, micro, m)

        @pl.when(kind == 0)
        def _():
            dispatch(m)

        @pl.when(kind == 1)
        def _():
            run_experts(m)

        @pl.when(kind == 2)
        def _():
            combine(m)

        return 0

    lax.fori_loop(0, len(order), stage, 0)

    @pl.when(section < sections - 1)
    def _():
        pltpu.make_async_copy(finished, finished, finished_sem).wait()

    packed = finished[...].astype(F32)
    result[0] = jnp.concatenate([packed[:rows], packed[rows:]], axis=1).astype(BF16)

    @pl.when(section != 0)
    def _():
        first_copy.wait_send()

    def drain(m, _):
        for source, semaphore in ((dispatched, dispatch_send), (produced, produce_send)):
            view = source.at[m, pl.ds(0, len(partners)), pl.ds(0, sent)]
            pltpu.make_async_copy(view, view, semaphore.at[m]).wait()

        @pl.when((section < sections - 1) | (m < micros - 1))
        def _():
            pltpu.make_async_copy(outgoing.at[m], outgoing.at[m], hidden_send.at[m]).wait()

        return 0

    lax.fori_loop(0, micros, drain, 0)


def solution(mesh):
    sections = mesh.shape["section"]
    experts = mesh.shape["expert"]
    grid_z = grid_x = int(round((experts // 2) ** 0.5))

    def per_device(tokens, norm_gain, router, w_gate, w_up, w_down, expert_ids):
        rows, width = tokens.shape[1:]
        inner_width = w_gate.shape[3]
        chunks = width // lane
        micros = expert_ids.shape[1]
        used = chunks * rows
        slots = experts * capacity
        messages = experts * message_rows
        vmem = pl.BlockSpec(memory_space=pltpu.VMEM)
        anywhere = pl.BlockSpec(memory_space=pl.ANY)
        dma = pltpu.SemaphoreType.DMA
        packed = (2 * rows, width // 2)
        return pl.pallas_call(
            functools.partial(kernel, grid_z, grid_x, sections, chunks),
            out_shape=jax.ShapeDtypeStruct(tokens.shape, BF16),
            in_specs=[vmem, vmem, vmem, anywhere, anywhere, anywhere, vmem],
            out_specs=vmem,
            scratch_shapes=[
                pltpu.VMEM((width, inner_width), BF16),
                pltpu.VMEM((width, inner_width), BF16),
                pltpu.VMEM((inner_width, width), BF16),
                pltpu.VMEM((micros,) + packed, BF16),
                pltpu.VMEM(packed, BF16),
                pltpu.VMEM(packed, BF16),
                pltpu.VMEM((micros,) + packed, BF16),
                pltpu.VMEM((micros, messages, 256), BF16),
                pltpu.VMEM((micros, capacity, rows, experts), F32),
                pltpu.VMEM((micros, chunks * 16, messages), BF16),
                pltpu.VMEM((micros, 256, lane), BF16),
                pltpu.VMEM((micros, experts, message_rows, lane), BF16),
                pltpu.VMEM((micros, experts, message_rows, lane), BF16),
                pltpu.VMEM((micros, experts, message_rows, lane), BF16),
                pltpu.VMEM((micros, experts, message_rows, lane), BF16),
                pltpu.VMEM((slots, width), BF16),
                pltpu.VMEM((slots, inner_width), BF16),
                pltpu.VMEM((experts // 4, 256, lane), BF16),
                pltpu.VMEM((used, 4 * message_rows), BF16),
                pltpu.VMEM((4 * message_rows, 256), BF16),
                pltpu.VMEM((capacity, experts, messages), BF16),
                pltpu.VMEM((chunks * 16, lane), BF16),
                dma, dma, dma,
                dma((micros,)), dma((micros,)), dma,
                dma((micros,)), dma((micros,)), dma((micros,)), dma((micros,)), dma,
            ],
            compiler_params=pltpu.CompilerParams(
                collective_id=0, has_side_effects=True, vmem_limit_bytes=58 * 2**20
            ),
            name="expert_layers",
        )(tokens, norm_gain, jnp.swapaxes(router, 1, 2), w_gate, w_up, w_down, expert_ids)

    placed = (
        P("section", "expert", None),
        P("section", None),
        P("section", None, None),
        P("section", "expert", None, None),
        P("section", "expert", None, None),
        P("section", "expert", None, None),
        P("section", None, "expert", None),
    )
    return jax.shard_map(
        per_device,
        mesh=mesh,
        in_specs=placed,
        out_specs=P("section", "expert", None),
        check_vma=False,
    )
```

```python
import functools

import jax
import jax.numpy as jnp
from jax import lax
from jax.experimental import pallas as pl
from jax.experimental.pallas import tpu as pltpu
from jax.sharding import PartitionSpec as P

MESH = pl.DeviceIdType.MESH
BF16 = jnp.bfloat16
F32 = jnp.float32

epsilon = 1e-06
routed_scale = 2.5
capacity = 2
lane = 128
part_chunks = 16
part_rows = part_chunks * capacity


def dot(a, b):
    return jnp.dot(a, b, preferred_element_type=F32)


def iota(shape, dim):
    return lax.broadcasted_iota(jnp.int32, shape, dim)


def ones_where(mask, dtype=BF16):
    return jnp.where(mask, 1.0, 0.0).astype(dtype)


def schedule(micros):
    order = []
    for m in range(0, micros, 2):
        if m:
            order += [(2, m - 2), (0, m), (2, m - 1), (0, m + 1), (1, m), (1, m + 1)]
        else:
            order += [(0, 0), (0, 1), (1, 0), (1, 1)]
    return order + [(2, micros - 2), (2, micros - 1)]


def kernel(
    grid_z, grid_x, sections, chunks, tokens, gain, router, w_gate, w_up, w_down, ids, result,
    gate_v, up_v, down_v, hidden, finished, staged, outgoing,
    place, pick, factors, stacked, dispatched, arrived, produced, returned,
    rows_in, gate_sum, up_sum, inner, columns, select, select_t, spread, mask_j,
    gate_sem, up_sem, down_sem, hidden_sem, hidden_send, finished_sem,
    dispatch_send, arrive_sem, produce_send, return_sem, local_sem,
):
    section = lax.axis_index("section")
    me = lax.axis_index("expert")
    experts = grid_z * grid_x * 2
    micros = sections
    rows = 8
    width = chunks * lane
    half = width // 2
    inner_width = gate_v.shape[1]
    core, x, z = lax.rem(me, 2), lax.rem(me // 2, grid_x), me // (2 * grid_x)

    def distance(step, size):
        return min(step, size - step)

    offsets = [(dz, dx, dc) for dz in range(grid_z) for dx in range(grid_x) for dc in range(2)]
    offsets.sort(key=lambda o: -(10 * (distance(o[0], grid_z) + distance(o[1], grid_x)) + o[2]))
    partners = []
    for dz, dx, dc in offsets[:-1]:
        partners.append(
            lax.rem(z + dz, grid_z) * (2 * grid_x) + lax.rem(x + dx, grid_x) * 2 + lax.rem(core + dc, 2)
        )

    copy_gate = pltpu.make_async_copy(w_gate.at[0, 0], gate_v, gate_sem)
    copy_up = pltpu.make_async_copy(w_up.at[0, 0], up_v, up_sem)
    copy_down = pltpu.make_async_copy(w_down.at[0, 0], down_v, down_sem)
    copy_gate.start()
    copy_up.start()
    copy_down.start()

    parts = [(0, part_chunks), (part_chunks, chunks)]
    sent = [(last - first) * capacity for first, last in parts]

    for room in (arrived, returned):
        for m in range(micros):
            room[m, 1, :, part_rows - 16 :, :] = jnp.zeros((experts, 16, lane), BF16)

    barrier = pltpu.get_barrier_semaphore()
    for partner in partners:
        pl.semaphore_signal(barrier, inc=1, device_id={"expert": partner}, device_id_type=MESH)
    for step in range(1, sections):
        pl.semaphore_signal(
            barrier, inc=1, device_id={"section": lax.rem(section + step, sections)}, device_id_type=MESH
        )

    tail = (chunks - part_chunks) * rows
    for m in range(micros):
        stacked[m, tail:, lane:] = jnp.zeros((part_chunks * rows - tail, lane), BF16)

    shape = (part_rows, lane)
    r, c = iota(shape, 0), iota(shape, 1)
    diagonal = [
        jnp.where((c // rows == r // capacity) & (r % capacity == p), 1.0, 0.0).astype(F32)
        for p in range(capacity)
    ]
    repeat = jnp.where(iota((rows, lane), 1) % rows == iota((rows, lane), 0), 1.0, 0.0).astype(F32)
    token_of = iota((rows, experts), 0)
    expert_of = iota((rows, experts), 1)

    def plan(m, _=0):
        choices = ids[0, m]
        hit = jnp.zeros((rows, experts), F32)
        for k in range(choices.shape[1]):
            hit = hit + jnp.where(choices[:, k : k + 1] == expert_of, 1.0, 0.0)
        before = jnp.zeros((rows, experts), F32)
        for t in range(rows - 1):
            before = before + jnp.where(token_of > t, 1.0, 0.0) * hit[t : t + 1, :]
        lanes = []
        for p in range(capacity):
            taken = jnp.where(before == float(p), hit, 0.0)
            pick[m, p] = taken
            lanes.append(
                lax.dot_general(taken, repeat, (((0,), (0,)), ((), ())), preferred_element_type=F32)
            )
        for e in range(experts):
            block = diagonal[0] * lanes[0][e : e + 1, :] + diagonal[1] * lanes[1][e : e + 1, :]
            place[m, e * part_rows : (e + 1) * part_rows, :] = block.astype(BF16)
        return 0

    def load_hidden(m):
        packed = hidden[m].astype(F32)
        return jnp.concatenate([packed[:rows], packed[rows:]], axis=1)

    def normalize(m):
        values = load_hidden(m)
        inverse_rms = lax.rsqrt(jnp.mean(values * values, axis=-1, keepdims=True) + epsilon)
        return values * inverse_rms * gain[...].astype(F32)

    def fill_slots(m):
        normed = normalize(m)
        for q, (first, last) in enumerate(parts):
            stacked[m, : (last - first) * rows, q * lane : (q + 1) * lane] = jnp.concatenate(
                [normed[:, j * lane : (j + 1) * lane] for j in range(first, last)], axis=0
            ).astype(BF16)
        slots = dot(place[m], stacked[m]).astype(BF16)
        for q in range(2):
            dispatched[m, q] = slots[:, q * lane : (q + 1) * lane].reshape(experts, part_rows, lane)

    def send(m, q, source, target, send_sem, receive_sem):
        for partner in partners:
            pltpu.make_async_remote_copy(
                src_ref=source.at[m, q, partner, pl.ds(0, sent[q])],
                dst_ref=target.at[m, q, me, pl.ds(0, sent[q])],
                send_sem=send_sem.at[m, q], recv_sem=receive_sem.at[m, q],
                device_id={"expert": partner}, device_id_type=MESH,
            ).start()
        pltpu.make_async_copy(
            source.at[m, q, me, pl.ds(0, sent[q])],
            target.at[m, q, me, pl.ds(0, sent[q])],
            receive_sem.at[m, q],
        ).start()

    def receive(m, q, target, receive_sem):
        view = target.at[m, q, :, pl.ds(0, sent[q])]
        pltpu.make_async_copy(view, view, receive_sem.at[m, q]).wait()

    def send_slots(m):
        for q in range(2):
            send(m, q, dispatched, arrived, dispatch_send, arrive_sem)

    def spread_factors(m):
        normed = normalize(m)
        twice = jnp.concatenate([normed, normed], axis=0).astype(BF16)
        logits = lax.dot_general(
            twice, router[0], (((1,), (1,)), ((), ())), preferred_element_type=F32
        )
        scores = jax.nn.sigmoid(logits[:rows])
        kept = [pick[m, p] for p in range(capacity)]
        chosen = jnp.zeros((rows, experts), F32)
        for k in range(ids.shape[3]):
            chosen = chosen + jnp.where(ids[0, m][:, k : k + 1] == expert_of, scores, 0.0)
        weights = routed_scale * scores / jnp.sum(chosen, axis=-1, keepdims=True)
        wide = None
        for p in range(capacity):
            factor = weights * kept[p]
            high = factor.astype(BF16).astype(F32)
            both = jnp.concatenate([high, factor - high], axis=0).astype(BF16)
            part = dot(both, spread[p])
            wide = part if wide is None else wide + part
        wide = wide.astype(BF16)
        for j in range(part_chunks):
            mask = mask_j[j * 16 : (j + 1) * 16, :]
            factors[m, j * 16 : (j + 1) * 16, :] = wide * jnp.concatenate(
                [mask] * (experts * part_rows // lane), axis=1
            )

    def dispatch(m):
        @pl.when((section != 0) | (m != 0))
        def _():
            pltpu.make_async_copy(hidden.at[m], hidden.at[m], hidden_sem.at[m]).wait()
            fill_slots(m)
            send_slots(m)

        spread_factors(m)

    def sort_rows(m, q):
        first, last = parts[q]
        for pair in range(experts // 16):
            both = [
                arrived[m, q, 16 * pair + 8 * i : 16 * pair + 8 * i + 8].reshape(8 * part_rows, lane)
                for i in range(2)
            ]
            ordered = dot(select[: (last - first) * 16, :], jnp.concatenate(both, axis=1)).astype(BF16)
            for j in range(first, last):
                tile = ordered[(j - first) * 16 : (j - first + 1) * 16, :]
                cols = slice(j * lane, (j + 1) * lane)
                rows_in[pair * 32 : pair * 32 + 16, cols] = tile[:, :lane]
                rows_in[pair * 32 + 16 : pair * 32 + 32, cols] = tile[:, lane:]

    def run_experts(m):
        split = part_chunks * lane
        receive(m, 0, arrived, arrive_sem)
        sort_rows(m, 0)

        @pl.when(m == 0)
        def _():
            copy_gate.wait()
            copy_up.wait()

        for n in range(inner_width // 256):
            cols = slice(n * 256, (n + 1) * 256)
            gate_sum[:, cols] = dot(rows_in[:, :split], gate_v[:split, cols])
            up_sum[:, cols] = dot(rows_in[:, :split], up_v[:split, cols])
        receive(m, 1, arrived, arrive_sem)
        sort_rows(m, 1)
        for n in range(inner_width // 256):
            cols = slice(n * 256, (n + 1) * 256)
            gate_part = gate_sum[:, cols] + dot(rows_in[:, split:], gate_v[split:, cols])
            up_part = up_sum[:, cols] + dot(rows_in[:, split:], up_v[split:, cols])
            inner[:, cols] = (gate_part / (1.0 + jnp.exp(-gate_part)) * up_part).astype(BF16)

        @pl.when(m == 0)
        def _():
            copy_down.wait()

        step = 4
        for q, (first, last) in enumerate(parts):
            for n in range(first, last, step):
                out = dot(inner[...], down_v[:, n * lane : (n + step) * lane]).astype(BF16)
                for g in range(experts // 8):
                    for j in range(step):
                        columns[q, g, (n - first + j) * 16 : (n - first + j + 1) * 16, :] = out[
                            g * 16 : (g + 1) * 16, j * lane : (j + 1) * lane
                        ]
            for pair in range(experts // 16):
                both = jnp.concatenate([columns[q, 2 * pair], columns[q, 2 * pair + 1]], axis=1)
                back = dot(select_t[...], both).astype(BF16)
                for i in range(2):
                    produced[m, q, 16 * pair + 8 * i : 16 * pair + 8 * i + 8] = back[
                        :, i * lane : (i + 1) * lane
                    ].reshape(8, part_rows, lane)
            send(m, q, produced, returned, produce_send, return_sem)

    def combine(m):
        for q in range(2):
            receive(m, q, returned, return_sem)
        both = [returned[m, q].reshape(experts * part_rows, lane) for q in range(2)]
        branch = dot(factors[m], jnp.concatenate(both, axis=1))
        values = load_hidden(m)
        fresh = []
        for j in range(chunks):
            q, row = j // part_chunks, (j % part_chunks) * 16
            cols = slice(q * lane, (q + 1) * lane)
            part = branch[row : row + 8, cols] + branch[row + 8 : row + 16, cols]
            fresh.append(values[:, j * lane : (j + 1) * lane] + part)
        split = chunks // 2
        outgoing[m] = jnp.concatenate(
            [jnp.concatenate(fresh[:split], axis=1), jnp.concatenate(fresh[split:], axis=1)], axis=0
        ).astype(BF16)

        @pl.when(section < sections - 1)
        def _():
            pltpu.make_async_remote_copy(
                src_ref=outgoing.at[m], dst_ref=hidden.at[m],
                send_sem=hidden_send.at[m], recv_sem=hidden_sem.at[m],
                device_id={"section": lax.rem(section + 1, sections)}, device_id_type=MESH,
            ).start()

        @pl.when((section == sections - 1) & (m < micros - 1))
        def _():
            pltpu.make_async_remote_copy(
                src_ref=outgoing.at[m], dst_ref=finished,
                send_sem=hidden_send.at[m], recv_sem=finished_sem,
                device_id={"section": lax.rem(m, sections)}, device_id_type=MESH,
            ).start()

        @pl.when((section == sections - 1) & (m == micros - 1))
        def _():
            finished[...] = outgoing[m]

    held = tokens[0].astype(F32)
    staged[...] = jnp.concatenate([held[:, :half], held[:, half:]], axis=0).astype(BF16)
    plan(0)

    @pl.when(section == 0)
    def _():
        hidden[0] = staged[...]
        fill_slots(0)

    pl.semaphore_wait(barrier, len(partners) + sections - 1)

    first_copy = pltpu.make_async_remote_copy(
        src_ref=staged, dst_ref=hidden.at[section], send_sem=local_sem, recv_sem=hidden_sem.at[section],
        device_id={"section": 0}, device_id_type=MESH,
    )

    @pl.when(section == 0)
    def _():
        send_slots(0)

    @pl.when(section != 0)
    def _():
        first_copy.start()

    shape = (8 * part_rows, 8 * part_rows)
    r, c = iota(shape, 0), iota(shape, 1)
    select[...] = ones_where(c == ((r % 16) // 2) * part_rows + (r // 16) * 2 + r % 2)
    select_t[...] = ones_where(r == ((c % 16) // 2) * part_rows + (c // 16) * 2 + c % 2)
    shape = (experts, experts * part_rows)
    r, c = iota(shape, 0), iota(shape, 1)
    for p in range(capacity):
        spread[p] = ones_where((c // part_rows == r) & (c % capacity == p))
    shape = (part_chunks * 16, lane)
    r, c = iota(shape, 0), iota(shape, 1)
    mask_j[...] = ones_where((c % part_rows) // capacity == r // 16)
    for g in range(experts // 8):
        columns[1, g, (chunks - part_chunks) * 16 :, :] = jnp.zeros(((2 * part_chunks - chunks) * 16, lane), BF16)
    lax.fori_loop(1, micros, plan, 0)

    order = schedule(micros)

    def stage(i, _):
        kind, m = jnp.int32(order[0][0]), jnp.int32(order[0][1])
        for index, (k, micro) in enumerate(order):
            kind = jnp.where(i == index, k, kind)
            m = jnp.where(i == index, micro, m)

        @pl.when(kind == 0)
        def _():
            dispatch(m)

        @pl.when(kind == 1)
        def _():
            run_experts(m)

        @pl.when(kind == 2)
        def _():
            combine(m)

        return 0

    lax.fori_loop(0, len(order), stage, 0)

    @pl.when(section < sections - 1)
    def _():
        pltpu.make_async_copy(finished, finished, finished_sem).wait()

    packed = finished[...].astype(F32)
    result[0] = jnp.concatenate([packed[:rows], packed[rows:]], axis=1).astype(BF16)

    @pl.when(section != 0)
    def _():
        first_copy.wait_send()

    def drain(m, _):
        for q in range(2):
            for source, semaphore in ((dispatched, dispatch_send), (produced, produce_send)):
                view = source.at[m, q, pl.ds(0, len(partners)), pl.ds(0, sent[q])]
                pltpu.make_async_copy(view, view, semaphore.at[m, q]).wait()

        @pl.when((section < sections - 1) | (m < micros - 1))
        def _():
            pltpu.make_async_copy(outgoing.at[m], outgoing.at[m], hidden_send.at[m]).wait()

        return 0

    lax.fori_loop(0, micros, drain, 0)


def solution(mesh):
    sections = mesh.shape["section"]
    experts = mesh.shape["expert"]
    grid_z = grid_x = int(round((experts // 2) ** 0.5))

    def per_device(tokens, norm_gain, router, w_gate, w_up, w_down, expert_ids):
        rows, width = tokens.shape[1:]
        inner_width = w_gate.shape[3]
        chunks = width // lane
        micros = expert_ids.shape[1]
        slots = experts * capacity
        messages = experts * part_rows
        vmem = pl.BlockSpec(memory_space=pltpu.VMEM)
        anywhere = pl.BlockSpec(memory_space=pl.ANY)
        dma = pltpu.SemaphoreType.DMA
        packed = (2 * rows, width // 2)
        return pl.pallas_call(
            functools.partial(kernel, grid_z, grid_x, sections, chunks),
            out_shape=jax.ShapeDtypeStruct(tokens.shape, BF16),
            in_specs=[vmem, vmem, vmem, anywhere, anywhere, anywhere, vmem],
            out_specs=vmem,
            scratch_shapes=[
                pltpu.VMEM((width, inner_width), BF16),
                pltpu.VMEM((width, inner_width), BF16),
                pltpu.VMEM((inner_width, width), BF16),
                pltpu.VMEM((micros,) + packed, BF16),
                pltpu.VMEM(packed, BF16),
                pltpu.VMEM(packed, BF16),
                pltpu.VMEM((micros,) + packed, BF16),
                pltpu.VMEM((micros, messages, lane), BF16),
                pltpu.VMEM((micros, capacity, rows, experts), F32),
                pltpu.VMEM((micros, part_chunks * 16, messages), BF16),
                pltpu.VMEM((micros, part_chunks * rows, 2 * lane), BF16),
                pltpu.VMEM((micros, 2, experts, part_rows, lane), BF16),
                pltpu.VMEM((micros, 2, experts, part_rows, lane), BF16),
                pltpu.VMEM((micros, 2, experts, part_rows, lane), BF16),
                pltpu.VMEM((micros, 2, experts, part_rows, lane), BF16),
                pltpu.VMEM((slots, width), BF16),
                pltpu.VMEM((slots, inner_width), F32),
                pltpu.VMEM((slots, inner_width), F32),
                pltpu.VMEM((slots, inner_width), BF16),
                pltpu.VMEM((2, experts // 8, part_chunks * 16, lane), BF16),
                pltpu.VMEM((8 * part_rows, 8 * part_rows), BF16),
                pltpu.VMEM((8 * part_rows, 8 * part_rows), BF16),
                pltpu.VMEM((capacity, experts, messages), BF16),
                pltpu.VMEM((part_chunks * 16, lane), BF16),
                dma, dma, dma,
                dma((micros,)), dma((micros,)), dma,
                dma((micros, 2)), dma((micros, 2)), dma((micros, 2)), dma((micros, 2)), dma,
            ],
            compiler_params=pltpu.CompilerParams(
                collective_id=0, has_side_effects=True, vmem_limit_bytes=58 * 2**20
            ),
            name="expert_layers",
        )(tokens, norm_gain, jnp.swapaxes(router, 1, 2), w_gate, w_up, w_down, expert_ids)

    placed = (
        P("section", "expert", None),
        P("section", None),
        P("section", None, None),
        P("section", "expert", None, None),
        P("section", "expert", None, None),
        P("section", "expert", None, None),
        P("section", None, "expert", None),
    )
    return jax.shard_map(
        per_device,
        mesh=mesh,
        in_specs=placed,
        out_specs=P("section", "expert", None),
        check_vma=False,
    )
```

```python
import functools

import jax
import jax.numpy as jnp
from jax import lax
from jax.experimental import pallas as pl
from jax.experimental.pallas import tpu as pltpu
from jax.sharding import PartitionSpec as P

MESH = pl.DeviceIdType.MESH
BF16 = jnp.bfloat16
F32 = jnp.float32

epsilon = 1e-06
routed_scale = 2.5
capacity = 2
lane = 128
part_chunks = 16
part_rows = part_chunks * capacity


def dot(a, b):
    return jnp.dot(a, b, preferred_element_type=F32)


def iota(shape, dim):
    return lax.broadcasted_iota(jnp.int32, shape, dim)


def ones_where(mask, dtype=BF16):
    return jnp.where(mask, 1.0, 0.0).astype(dtype)


def schedule(micros):
    order = []
    for m in range(0, micros, 2):
        if m:
            order += [(2, m - 2), (0, m), (2, m - 1), (0, m + 1), (1, m), (1, m + 1)]
        else:
            order += [(0, 0), (0, 1), (1, 0), (1, 1)]
    return order + [(2, micros - 2), (2, micros - 1)]


def kernel(
    grid_z, grid_x, sections, chunks, tokens, gain, router, w_gate, w_up, w_down, ids, result,
    gate_v, up_v, down_v, hidden, finished, staged, outgoing,
    place, pick, factors, stacked, dispatched, arrived, produced, returned,
    rows_in, gate_sum, up_sum, inner, columns, select, select_t, spread, mask_j,
    gate_sem, up_sem, down_sem, hidden_sem, hidden_send, finished_sem,
    dispatch_send, arrive_sem, produce_send, return_sem, local_sem,
):
    section = lax.axis_index("section")
    me = lax.axis_index("expert")
    experts = grid_z * grid_x * 2
    micros = sections
    rows = 8
    width = chunks * lane
    half = width // 2
    inner_width = gate_v.shape[1]
    core, x, z = lax.rem(me, 2), lax.rem(me // 2, grid_x), me // (2 * grid_x)

    def distance(step, size):
        return min(step, size - step)

    offsets = [(da, db, dc) for dc in range(2) for da in range(grid_z) for db in range(grid_x)]
    offsets.sort(key=lambda o: -(distance(o[0], grid_z) + distance(o[1], grid_x)))
    partners = []
    for da, db, dc in offsets:
        if (da, db, dc) == (0, 0, 0):
            continue
        dz, dx = jnp.where(core == 0, da, db), jnp.where(core == 0, db, da)
        partners.append(
            lax.rem(z + dz, grid_z) * (2 * grid_x) + lax.rem(x + dx, grid_x) * 2 + lax.rem(core + dc, 2)
        )

    copy_gate = pltpu.make_async_copy(w_gate.at[0, 0], gate_v, gate_sem)
    copy_up = pltpu.make_async_copy(w_up.at[0, 0], up_v, up_sem)
    copy_down = pltpu.make_async_copy(w_down.at[0, 0], down_v, down_sem)
    copy_gate.start()
    copy_up.start()
    copy_down.start()

    parts = [(0, part_chunks), (part_chunks, chunks)]
    sent = [(last - first) * capacity for first, last in parts]

    for room in (arrived, returned):
        for m in range(micros):
            room[m, 1, :, part_rows - 16 :, :] = jnp.zeros((experts, 16, lane), BF16)

    barrier = pltpu.get_barrier_semaphore()
    for partner in partners:
        pl.semaphore_signal(barrier, inc=1, device_id={"expert": partner}, device_id_type=MESH)
    for step in range(1, sections):
        pl.semaphore_signal(
            barrier, inc=1, device_id={"section": lax.rem(section + step, sections)}, device_id_type=MESH
        )

    tail = (chunks - part_chunks) * rows
    for m in range(micros):
        stacked[m, tail:, lane:] = jnp.zeros((part_chunks * rows - tail, lane), BF16)

    shape = (part_rows, lane)
    r, c = iota(shape, 0), iota(shape, 1)
    diagonal = [
        jnp.where((c // rows == r // capacity) & (r % capacity == p), 1.0, 0.0).astype(F32)
        for p in range(capacity)
    ]
    repeat = jnp.where(iota((rows, lane), 1) % rows == iota((rows, lane), 0), 1.0, 0.0).astype(F32)
    token_of = iota((rows, experts), 0)
    expert_of = iota((rows, experts), 1)

    def plan(m, _=0):
        choices = ids[0, m]
        hit = jnp.zeros((rows, experts), F32)
        for k in range(choices.shape[1]):
            hit = hit + jnp.where(choices[:, k : k + 1] == expert_of, 1.0, 0.0)
        before = jnp.zeros((rows, experts), F32)
        for t in range(rows - 1):
            before = before + jnp.where(token_of > t, 1.0, 0.0) * hit[t : t + 1, :]
        lanes = []
        for p in range(capacity):
            taken = jnp.where(before == float(p), hit, 0.0)
            pick[m, p] = taken
            lanes.append(
                lax.dot_general(taken, repeat, (((0,), (0,)), ((), ())), preferred_element_type=F32)
            )
        for e in range(experts):
            block = diagonal[0] * lanes[0][e : e + 1, :] + diagonal[1] * lanes[1][e : e + 1, :]
            place[m, e * part_rows : (e + 1) * part_rows, :] = block.astype(BF16)
        return 0

    def load_hidden(m):
        packed = hidden[m].astype(F32)
        return jnp.concatenate([packed[:rows], packed[rows:]], axis=1)

    def normalize(m):
        values = load_hidden(m)
        inverse_rms = lax.rsqrt(jnp.mean(values * values, axis=-1, keepdims=True) + epsilon)
        return values * inverse_rms * gain[...].astype(F32)

    def fill_slots(m):
        normed = normalize(m)
        for q, (first, last) in enumerate(parts):
            stacked[m, : (last - first) * rows, q * lane : (q + 1) * lane] = jnp.concatenate(
                [normed[:, j * lane : (j + 1) * lane] for j in range(first, last)], axis=0
            ).astype(BF16)
        slots = dot(place[m], stacked[m]).astype(BF16)
        for q in range(2):
            dispatched[m, q] = slots[:, q * lane : (q + 1) * lane].reshape(experts, part_rows, lane)

    def send(m, q, source, target, send_sem, receive_sem):
        for partner in partners:
            pltpu.make_async_remote_copy(
                src_ref=source.at[m, q, partner, pl.ds(0, sent[q])],
                dst_ref=target.at[m, q, me, pl.ds(0, sent[q])],
                send_sem=send_sem.at[m, q], recv_sem=receive_sem.at[m, q],
                device_id={"expert": partner}, device_id_type=MESH,
            ).start()
        pltpu.make_async_copy(
            source.at[m, q, me, pl.ds(0, sent[q])],
            target.at[m, q, me, pl.ds(0, sent[q])],
            receive_sem.at[m, q],
        ).start()

    def receive(m, q, target, receive_sem):
        view = target.at[m, q, :, pl.ds(0, sent[q])]
        pltpu.make_async_copy(view, view, receive_sem.at[m, q]).wait()

    def send_slots(m):
        for q in range(2):
            send(m, q, dispatched, arrived, dispatch_send, arrive_sem)

    def spread_factors(m):
        normed = normalize(m)
        twice = jnp.concatenate([normed, normed], axis=0).astype(BF16)
        logits = lax.dot_general(
            twice, router[0], (((1,), (1,)), ((), ())), preferred_element_type=F32
        )
        scores = jax.nn.sigmoid(logits[:rows])
        kept = [pick[m, p] for p in range(capacity)]
        chosen = jnp.zeros((rows, experts), F32)
        for k in range(ids.shape[3]):
            chosen = chosen + jnp.where(ids[0, m][:, k : k + 1] == expert_of, scores, 0.0)
        weights = routed_scale * scores / jnp.sum(chosen, axis=-1, keepdims=True)
        wide = None
        for p in range(capacity):
            factor = weights * kept[p]
            high = factor.astype(BF16).astype(F32)
            both = jnp.concatenate([high, factor - high], axis=0).astype(BF16)
            part = dot(both, spread[p])
            wide = part if wide is None else wide + part
        wide = wide.astype(BF16)
        for j in range(part_chunks):
            mask = mask_j[j * 16 : (j + 1) * 16, :]
            factors[m, j * 16 : (j + 1) * 16, :] = wide * jnp.concatenate(
                [mask] * (experts * part_rows // lane), axis=1
            )

    def dispatch(m):
        @pl.when((section != 0) | (m != 0))
        def _():
            pltpu.make_async_copy(hidden.at[m], hidden.at[m], hidden_sem.at[m]).wait()
            fill_slots(m)
            send_slots(m)

        spread_factors(m)

    def sort_rows(m, q):
        first, last = parts[q]
        for pair in range(experts // 16):
            both = [
                arrived[m, q, 16 * pair + 8 * i : 16 * pair + 8 * i + 8].reshape(8 * part_rows, lane)
                for i in range(2)
            ]
            ordered = dot(select[: (last - first) * 16, :], jnp.concatenate(both, axis=1)).astype(BF16)
            for j in range(first, last):
                tile = ordered[(j - first) * 16 : (j - first + 1) * 16, :]
                cols = slice(j * lane, (j + 1) * lane)
                rows_in[pair * 32 : pair * 32 + 16, cols] = tile[:, :lane]
                rows_in[pair * 32 + 16 : pair * 32 + 32, cols] = tile[:, lane:]

    def run_experts(m):
        split = part_chunks * lane
        receive(m, 0, arrived, arrive_sem)
        sort_rows(m, 0)

        @pl.when(m == 0)
        def _():
            copy_gate.wait()
            copy_up.wait()

        for n in range(inner_width // 256):
            cols = slice(n * 256, (n + 1) * 256)
            gate_sum[:, cols] = dot(rows_in[:, :split], gate_v[:split, cols])
            up_sum[:, cols] = dot(rows_in[:, :split], up_v[:split, cols])
        receive(m, 1, arrived, arrive_sem)
        sort_rows(m, 1)
        for n in range(inner_width // 256):
            cols = slice(n * 256, (n + 1) * 256)
            gate_part = gate_sum[:, cols] + dot(rows_in[:, split:], gate_v[split:, cols])
            up_part = up_sum[:, cols] + dot(rows_in[:, split:], up_v[split:, cols])
            inner[:, cols] = (gate_part / (1.0 + jnp.exp(-gate_part)) * up_part).astype(BF16)

        @pl.when(m == 0)
        def _():
            copy_down.wait()

        step = 4
        for q, (first, last) in reversed(list(enumerate(parts))):
            for n in range(first, last, step):
                out = dot(inner[...], down_v[:, n * lane : (n + step) * lane]).astype(BF16)
                for g in range(experts // 8):
                    for j in range(step):
                        columns[q, g, (n - first + j) * 16 : (n - first + j + 1) * 16, :] = out[
                            g * 16 : (g + 1) * 16, j * lane : (j + 1) * lane
                        ]
            for pair in range(experts // 16):
                both = jnp.concatenate([columns[q, 2 * pair], columns[q, 2 * pair + 1]], axis=1)
                back = dot(select_t[...], both).astype(BF16)
                for i in range(2):
                    produced[m, q, 16 * pair + 8 * i : 16 * pair + 8 * i + 8] = back[
                        :, i * lane : (i + 1) * lane
                    ].reshape(8, part_rows, lane)
            send(m, q, produced, returned, produce_send, return_sem)

    def combine(m):
        branch = [None, None]
        for q in (1, 0):
            receive(m, q, returned, return_sem)
            branch[q] = dot(factors[m], returned[m, q].reshape(experts * part_rows, lane))
        values = load_hidden(m)
        fresh = []
        for j in range(chunks):
            q, row = j // part_chunks, (j % part_chunks) * 16
            part = branch[q][row : row + 8, :] + branch[q][row + 8 : row + 16, :]
            fresh.append(values[:, j * lane : (j + 1) * lane] + part)
        split = chunks // 2
        outgoing[m] = jnp.concatenate(
            [jnp.concatenate(fresh[:split], axis=1), jnp.concatenate(fresh[split:], axis=1)], axis=0
        ).astype(BF16)

        @pl.when(section < sections - 1)
        def _():
            pltpu.make_async_remote_copy(
                src_ref=outgoing.at[m], dst_ref=hidden.at[m],
                send_sem=hidden_send.at[m], recv_sem=hidden_sem.at[m],
                device_id={"section": lax.rem(section + 1, sections)}, device_id_type=MESH,
            ).start()

        @pl.when((section == sections - 1) & (m < micros - 1))
        def _():
            pltpu.make_async_remote_copy(
                src_ref=outgoing.at[m], dst_ref=finished,
                send_sem=hidden_send.at[m], recv_sem=finished_sem,
                device_id={"section": lax.rem(m, sections)}, device_id_type=MESH,
            ).start()

        @pl.when((section == sections - 1) & (m == micros - 1))
        def _():
            finished[...] = outgoing[m]

    held = tokens[0].astype(F32)
    staged[...] = jnp.concatenate([held[:, :half], held[:, half:]], axis=0).astype(BF16)
    plan(0)

    @pl.when(section == 0)
    def _():
        hidden[0] = staged[...]
        fill_slots(0)

    pl.semaphore_wait(barrier, len(partners) + sections - 1)

    first_copy = pltpu.make_async_remote_copy(
        src_ref=staged, dst_ref=hidden.at[section], send_sem=local_sem, recv_sem=hidden_sem.at[section],
        device_id={"section": 0}, device_id_type=MESH,
    )

    @pl.when(section == 0)
    def _():
        send_slots(0)

    @pl.when(section != 0)
    def _():
        first_copy.start()

    shape = (8 * part_rows, 8 * part_rows)
    r, c = iota(shape, 0), iota(shape, 1)
    select[...] = ones_where(c == ((r % 16) // 2) * part_rows + (r // 16) * 2 + r % 2)
    select_t[...] = ones_where(r == ((c % 16) // 2) * part_rows + (c // 16) * 2 + c % 2)
    shape = (experts, experts * part_rows)
    r, c = iota(shape, 0), iota(shape, 1)
    for p in range(capacity):
        spread[p] = ones_where((c // part_rows == r) & (c % capacity == p))
    shape = (part_chunks * 16, lane)
    r, c = iota(shape, 0), iota(shape, 1)
    mask_j[...] = ones_where((c % part_rows) // capacity == r // 16)
    for g in range(experts // 8):
        columns[1, g, (chunks - part_chunks) * 16 :, :] = jnp.zeros(((2 * part_chunks - chunks) * 16, lane), BF16)
    lax.fori_loop(1, micros, plan, 0)

    order = schedule(micros)

    def stage(i, _):
        kind, m = jnp.int32(order[0][0]), jnp.int32(order[0][1])
        for index, (k, micro) in enumerate(order):
            kind = jnp.where(i == index, k, kind)
            m = jnp.where(i == index, micro, m)

        @pl.when(kind == 0)
        def _():
            dispatch(m)

        @pl.when(kind == 1)
        def _():
            run_experts(m)

        @pl.when(kind == 2)
        def _():
            combine(m)

        return 0

    lax.fori_loop(0, len(order), stage, 0)

    @pl.when(section < sections - 1)
    def _():
        pltpu.make_async_copy(finished, finished, finished_sem).wait()

    packed = finished[...].astype(F32)
    result[0] = jnp.concatenate([packed[:rows], packed[rows:]], axis=1).astype(BF16)

    @pl.when(section != 0)
    def _():
        first_copy.wait_send()

    def drain(m, _):
        for q in range(2):
            for source, semaphore in ((dispatched, dispatch_send), (produced, produce_send)):
                view = source.at[m, q, pl.ds(0, len(partners)), pl.ds(0, sent[q])]
                pltpu.make_async_copy(view, view, semaphore.at[m, q]).wait()

        @pl.when((section < sections - 1) | (m < micros - 1))
        def _():
            pltpu.make_async_copy(outgoing.at[m], outgoing.at[m], hidden_send.at[m]).wait()

        return 0

    lax.fori_loop(0, micros, drain, 0)


def solution(mesh):
    sections = mesh.shape["section"]
    experts = mesh.shape["expert"]
    grid_z = grid_x = int(round((experts // 2) ** 0.5))

    def per_device(tokens, norm_gain, router, w_gate, w_up, w_down, expert_ids):
        rows, width = tokens.shape[1:]
        inner_width = w_gate.shape[3]
        chunks = width // lane
        micros = expert_ids.shape[1]
        slots = experts * capacity
        messages = experts * part_rows
        vmem = pl.BlockSpec(memory_space=pltpu.VMEM)
        anywhere = pl.BlockSpec(memory_space=pl.ANY)
        dma = pltpu.SemaphoreType.DMA
        packed = (2 * rows, width // 2)
        return pl.pallas_call(
            functools.partial(kernel, grid_z, grid_x, sections, chunks),
            out_shape=jax.ShapeDtypeStruct(tokens.shape, BF16),
            in_specs=[vmem, vmem, vmem, anywhere, anywhere, anywhere, vmem],
            out_specs=vmem,
            scratch_shapes=[
                pltpu.VMEM((width, inner_width), BF16),
                pltpu.VMEM((width, inner_width), BF16),
                pltpu.VMEM((inner_width, width), BF16),
                pltpu.VMEM((micros,) + packed, BF16),
                pltpu.VMEM(packed, BF16),
                pltpu.VMEM(packed, BF16),
                pltpu.VMEM((micros,) + packed, BF16),
                pltpu.VMEM((micros, messages, lane), BF16),
                pltpu.VMEM((micros, capacity, rows, experts), F32),
                pltpu.VMEM((micros, part_chunks * 16, messages), BF16),
                pltpu.VMEM((micros, part_chunks * rows, 2 * lane), BF16),
                pltpu.VMEM((micros, 2, experts, part_rows, lane), BF16),
                pltpu.VMEM((micros, 2, experts, part_rows, lane), BF16),
                pltpu.VMEM((micros, 2, experts, part_rows, lane), BF16),
                pltpu.VMEM((micros, 2, experts, part_rows, lane), BF16),
                pltpu.VMEM((slots, width), BF16),
                pltpu.VMEM((slots, inner_width), F32),
                pltpu.VMEM((slots, inner_width), F32),
                pltpu.VMEM((slots, inner_width), BF16),
                pltpu.VMEM((2, experts // 8, part_chunks * 16, lane), BF16),
                pltpu.VMEM((8 * part_rows, 8 * part_rows), BF16),
                pltpu.VMEM((8 * part_rows, 8 * part_rows), BF16),
                pltpu.VMEM((capacity, experts, messages), BF16),
                pltpu.VMEM((part_chunks * 16, lane), BF16),
                dma, dma, dma,
                dma((micros,)), dma((micros,)), dma,
                dma((micros, 2)), dma((micros, 2)), dma((micros, 2)), dma((micros, 2)), dma,
            ],
            compiler_params=pltpu.CompilerParams(
                collective_id=0, has_side_effects=True, vmem_limit_bytes=58 * 2**20
            ),
            name="expert_layers",
        )(tokens, norm_gain, jnp.swapaxes(router, 1, 2), w_gate, w_up, w_down, expert_ids)

    placed = (
        P("section", "expert", None),
        P("section", None),
        P("section", None, None),
        P("section", "expert", None, None),
        P("section", "expert", None, None),
        P("section", "expert", None, None),
        P("section", None, "expert", None),
    )
    return jax.shard_map(
        per_device,
        mesh=mesh,
        in_specs=placed,
        out_specs=P("section", "expert", None),
        check_vma=False,
    )
```

```python
import functools

import jax
import jax.numpy as jnp
from jax import lax
from jax.experimental import pallas as pl
from jax.experimental.pallas import tpu as pltpu
from jax.sharding import PartitionSpec as P

MESH = pl.DeviceIdType.MESH
BF16 = jnp.bfloat16
F32 = jnp.float32

epsilon = 1e-06
routed_scale = 2.5
capacity = 2
lane = 128
part_chunks = 16
part_rows = part_chunks * capacity


def dot(a, b):
    return jnp.dot(a, b, preferred_element_type=F32)


def iota(shape, dim):
    return lax.broadcasted_iota(jnp.int32, shape, dim)


def ones_where(mask, dtype=BF16):
    return jnp.where(mask, 1.0, 0.0).astype(dtype)


def schedule(micros):
    order = []
    for m in range(0, micros, 2):
        if m:
            order += [(2, m - 2), (0, m), (2, m - 1), (0, m + 1), (1, m), (1, m + 1)]
        else:
            order += [(0, 0), (0, 1), (1, 0), (1, 1)]
    return order + [(2, micros - 2), (2, micros - 1)]


def kernel(
    grid_z, grid_x, sections, chunks, tokens, gain, router, w_gate, w_up, w_down, ids, result,
    gate_v, up_v, down_v, hidden_a, hidden_b, finished_a, finished_b, staged_a, staged_b, outgoing_a, outgoing_b,
    place, pick, factors, stacked, dispatched, arrived, produced, returned,
    rows_in, gate_sum, up_sum, inner, columns, select, select_t, spread, mask_j,
    gate_sem, up_sem, down_sem, hidden_sem, hidden_send, finished_sem,
    dispatch_send, arrive_sem, produce_send, return_sem, local_sem,
):
    section = lax.axis_index("section")
    me = lax.axis_index("expert")
    experts = grid_z * grid_x * 2
    micros = sections
    rows = 8
    width = chunks * lane
    inner_width = gate_v.shape[1]
    core, x, z = lax.rem(me, 2), lax.rem(me // 2, grid_x), me // (2 * grid_x)

    def distance(step, size):
        return min(step, size - step)

    offsets = [(da, db, dc) for dc in range(2) for da in range(grid_z) for db in range(grid_x)]
    offsets.sort(key=lambda o: -(distance(o[0], grid_z) + distance(o[1], grid_x)))
    partners = []
    for da, db, dc in offsets:
        if (da, db, dc) == (0, 0, 0):
            continue
        dz, dx = jnp.where(core == 0, da, db), jnp.where(core == 0, db, da)
        partners.append(
            lax.rem(z + dz, grid_z) * (2 * grid_x) + lax.rem(x + dx, grid_x) * 2 + lax.rem(core + dc, 2)
        )

    copy_gate = pltpu.make_async_copy(w_gate.at[0, 0], gate_v, gate_sem)
    copy_up = pltpu.make_async_copy(w_up.at[0, 0], up_v, up_sem)
    copy_down = pltpu.make_async_copy(w_down.at[0, 0], down_v, down_sem)
    copy_gate.start()
    copy_up.start()
    copy_down.start()

    hidden, finished = (hidden_a, hidden_b), (finished_a, finished_b)
    staged, outgoing = (staged_a, staged_b), (outgoing_a, outgoing_b)
    parts = [(0, part_chunks), (part_chunks, chunks)]
    sent = [(last - first) * capacity for first, last in parts]

    for room in (arrived, returned):
        for m in range(micros):
            room[m, 1, :, part_rows - 16 :, :] = jnp.zeros((experts, 16, lane), BF16)

    barrier = pltpu.get_barrier_semaphore()
    for partner in partners:
        pl.semaphore_signal(barrier, inc=1, device_id={"expert": partner}, device_id_type=MESH)
    for step in range(1, sections):
        pl.semaphore_signal(
            barrier, inc=1, device_id={"section": lax.rem(section + step, sections)}, device_id_type=MESH
        )

    tail = (chunks - part_chunks) * rows
    for m in range(micros):
        stacked[m, tail:, lane:] = jnp.zeros((part_chunks * rows - tail, lane), BF16)

    shape = (part_rows, lane)
    r, c = iota(shape, 0), iota(shape, 1)
    diagonal = [
        jnp.where((c // rows == r // capacity) & (r % capacity == p), 1.0, 0.0).astype(F32)
        for p in range(capacity)
    ]
    repeat = jnp.where(iota((rows, lane), 1) % rows == iota((rows, lane), 0), 1.0, 0.0).astype(F32)
    token_of = iota((rows, experts), 0)
    expert_of = iota((rows, experts), 1)

    def plan(m, _=0):
        choices = ids[0, m]
        hit = jnp.zeros((rows, experts), F32)
        for k in range(choices.shape[1]):
            hit = hit + jnp.where(choices[:, k : k + 1] == expert_of, 1.0, 0.0)
        before = jnp.zeros((rows, experts), F32)
        for t in range(rows - 1):
            before = before + jnp.where(token_of > t, 1.0, 0.0) * hit[t : t + 1, :]
        lanes = []
        for p in range(capacity):
            taken = jnp.where(before == float(p), hit, 0.0)
            pick[m, p] = taken
            lanes.append(
                lax.dot_general(taken, repeat, (((0,), (0,)), ((), ())), preferred_element_type=F32)
            )
        for e in range(experts):
            block = diagonal[0] * lanes[0][e : e + 1, :] + diagonal[1] * lanes[1][e : e + 1, :]
            place[m, e * part_rows : (e + 1) * part_rows, :] = block.astype(BF16)
        return 0

    def fold(part):
        middle = part.shape[1] // 2
        return jnp.concatenate([part[:, :middle], part[:, middle:]], axis=0).astype(BF16)

    def unfold(refs):
        pieces = []
        for packed in refs:
            packed = packed.astype(F32)
            pieces += [packed[:rows], packed[rows:]]
        return jnp.concatenate(pieces, axis=1)

    def load_hidden(m):
        return unfold([hidden[q][m] for q in range(2)])

    def normalize(m):
        values = load_hidden(m)
        inverse_rms = lax.rsqrt(jnp.mean(values * values, axis=-1, keepdims=True) + epsilon)
        return values * inverse_rms * gain[...].astype(F32)

    def fill_slots(m):
        normed = normalize(m)
        for q, (first, last) in enumerate(parts):
            stacked[m, : (last - first) * rows, q * lane : (q + 1) * lane] = jnp.concatenate(
                [normed[:, j * lane : (j + 1) * lane] for j in range(first, last)], axis=0
            ).astype(BF16)
        slots = dot(place[m], stacked[m]).astype(BF16)
        for q in range(2):
            dispatched[m, q] = slots[:, q * lane : (q + 1) * lane].reshape(experts, part_rows, lane)

    def send(m, q, source, target, send_sem, receive_sem):
        for partner in partners:
            pltpu.make_async_remote_copy(
                src_ref=source.at[m, q, partner, pl.ds(0, sent[q])],
                dst_ref=target.at[m, q, me, pl.ds(0, sent[q])],
                send_sem=send_sem.at[m, q], recv_sem=receive_sem.at[m, q],
                device_id={"expert": partner}, device_id_type=MESH,
            ).start()
        pltpu.make_async_copy(
            source.at[m, q, me, pl.ds(0, sent[q])],
            target.at[m, q, me, pl.ds(0, sent[q])],
            receive_sem.at[m, q],
        ).start()

    def receive(m, q, target, receive_sem):
        view = target.at[m, q, :, pl.ds(0, sent[q])]
        pltpu.make_async_copy(view, view, receive_sem.at[m, q]).wait()

    def send_slots(m):
        for q in range(2):
            send(m, q, dispatched, arrived, dispatch_send, arrive_sem)

    def spread_factors(m):
        normed = normalize(m)
        twice = jnp.concatenate([normed, normed], axis=0).astype(BF16)
        logits = lax.dot_general(
            twice, router[0], (((1,), (1,)), ((), ())), preferred_element_type=F32
        )
        scores = jax.nn.sigmoid(logits[:rows])
        kept = [pick[m, p] for p in range(capacity)]
        chosen = jnp.zeros((rows, experts), F32)
        for k in range(ids.shape[3]):
            chosen = chosen + jnp.where(ids[0, m][:, k : k + 1] == expert_of, scores, 0.0)
        weights = routed_scale * scores / jnp.sum(chosen, axis=-1, keepdims=True)
        wide = None
        for p in range(capacity):
            factor = weights * kept[p]
            high = factor.astype(BF16).astype(F32)
            both = jnp.concatenate([high, factor - high], axis=0).astype(BF16)
            part = dot(both, spread[p])
            wide = part if wide is None else wide + part
        wide = wide.astype(BF16)
        for j in range(part_chunks):
            mask = mask_j[j * 16 : (j + 1) * 16, :]
            factors[m, j * 16 : (j + 1) * 16, :] = wide * jnp.concatenate(
                [mask] * (experts * part_rows // lane), axis=1
            )

    def dispatch(m):
        @pl.when((section != 0) | (m != 0))
        def _():
            for q in (1, 0):
                pltpu.make_async_copy(hidden[q].at[m], hidden[q].at[m], hidden_sem.at[m, q]).wait()
            fill_slots(m)
            send_slots(m)

        spread_factors(m)

    def sort_rows(m, q):
        first, last = parts[q]
        for pair in range(experts // 16):
            both = [
                arrived[m, q, 16 * pair + 8 * i : 16 * pair + 8 * i + 8].reshape(8 * part_rows, lane)
                for i in range(2)
            ]
            ordered = dot(select[: (last - first) * 16, :], jnp.concatenate(both, axis=1)).astype(BF16)
            for j in range(first, last):
                tile = ordered[(j - first) * 16 : (j - first + 1) * 16, :]
                cols = slice(j * lane, (j + 1) * lane)
                rows_in[pair * 32 : pair * 32 + 16, cols] = tile[:, :lane]
                rows_in[pair * 32 + 16 : pair * 32 + 32, cols] = tile[:, lane:]

    def run_experts(m):
        split = part_chunks * lane
        receive(m, 0, arrived, arrive_sem)
        sort_rows(m, 0)

        @pl.when(m == 0)
        def _():
            copy_gate.wait()
            copy_up.wait()

        for n in range(inner_width // 256):
            cols = slice(n * 256, (n + 1) * 256)
            gate_sum[:, cols] = dot(rows_in[:, :split], gate_v[:split, cols])
            up_sum[:, cols] = dot(rows_in[:, :split], up_v[:split, cols])
        receive(m, 1, arrived, arrive_sem)
        sort_rows(m, 1)
        for n in range(inner_width // 256):
            cols = slice(n * 256, (n + 1) * 256)
            gate_part = gate_sum[:, cols] + dot(rows_in[:, split:], gate_v[split:, cols])
            up_part = up_sum[:, cols] + dot(rows_in[:, split:], up_v[split:, cols])
            inner[:, cols] = (gate_part / (1.0 + jnp.exp(-gate_part)) * up_part).astype(BF16)

        @pl.when(m == 0)
        def _():
            copy_down.wait()

        step = 4
        for q, (first, last) in reversed(list(enumerate(parts))):
            for n in range(first, last, step):
                out = dot(inner[...], down_v[:, n * lane : (n + step) * lane]).astype(BF16)
                for g in range(experts // 8):
                    for j in range(step):
                        columns[q, g, (n - first + j) * 16 : (n - first + j + 1) * 16, :] = out[
                            g * 16 : (g + 1) * 16, j * lane : (j + 1) * lane
                        ]
            for pair in range(experts // 16):
                both = jnp.concatenate([columns[q, 2 * pair], columns[q, 2 * pair + 1]], axis=1)
                back = dot(select_t[...], both).astype(BF16)
                for i in range(2):
                    produced[m, q, 16 * pair + 8 * i : 16 * pair + 8 * i + 8] = back[
                        :, i * lane : (i + 1) * lane
                    ].reshape(8, part_rows, lane)
            send(m, q, produced, returned, produce_send, return_sem)

    def combine(m):
        for q in (1, 0):
            first, last = parts[q]
            receive(m, q, returned, return_sem)
            branch = dot(factors[m], returned[m, q].reshape(experts * part_rows, lane))
            values = unfold([hidden[q][m]])
            fresh = []
            for j in range(last - first):
                part = branch[j * 16 : j * 16 + 8, :] + branch[j * 16 + 8 : j * 16 + 16, :]
                fresh.append(values[:, j * lane : (j + 1) * lane] + part)
            outgoing[q][m] = fold(jnp.concatenate(fresh, axis=1))
            pass_on(m, q)

    def pass_on(m, q):
        @pl.when(section < sections - 1)
        def _():
            pltpu.make_async_remote_copy(
                src_ref=outgoing[q].at[m], dst_ref=hidden[q].at[m],
                send_sem=hidden_send.at[m, q], recv_sem=hidden_sem.at[m, q],
                device_id={"section": lax.rem(section + 1, sections)}, device_id_type=MESH,
            ).start()

        @pl.when((section == sections - 1) & (m < micros - 1))
        def _():
            pltpu.make_async_remote_copy(
                src_ref=outgoing[q].at[m], dst_ref=finished[q],
                send_sem=hidden_send.at[m, q], recv_sem=finished_sem.at[q],
                device_id={"section": lax.rem(m, sections)}, device_id_type=MESH,
            ).start()

        @pl.when((section == sections - 1) & (m == micros - 1))
        def _():
            finished[q][...] = outgoing[q][m]

    held = tokens[0].astype(F32)
    for q, (first, last) in enumerate(parts):
        staged[q][...] = fold(held[:, first * lane : last * lane])
    plan(0)

    @pl.when(section == 0)
    def _():
        for q in range(2):
            hidden[q][0] = staged[q][...]
        fill_slots(0)

    pl.semaphore_wait(barrier, len(partners) + sections - 1)

    first_copies = [
        pltpu.make_async_remote_copy(
            src_ref=staged[q], dst_ref=hidden[q].at[section],
            send_sem=local_sem.at[q], recv_sem=hidden_sem.at[section, q],
            device_id={"section": 0}, device_id_type=MESH,
        )
        for q in range(2)
    ]

    @pl.when(section == 0)
    def _():
        send_slots(0)

    @pl.when(section != 0)
    def _():
        for copy in first_copies:
            copy.start()

    shape = (8 * part_rows, 8 * part_rows)
    r, c = iota(shape, 0), iota(shape, 1)
    select[...] = ones_where(c == ((r % 16) // 2) * part_rows + (r // 16) * 2 + r % 2)
    select_t[...] = ones_where(r == ((c % 16) // 2) * part_rows + (c // 16) * 2 + c % 2)
    shape = (experts, experts * part_rows)
    r, c = iota(shape, 0), iota(shape, 1)
    for p in range(capacity):
        spread[p] = ones_where((c // part_rows == r) & (c % capacity == p))
    shape = (part_chunks * 16, lane)
    r, c = iota(shape, 0), iota(shape, 1)
    mask_j[...] = ones_where((c % part_rows) // capacity == r // 16)
    for g in range(experts // 8):
        columns[1, g, (chunks - part_chunks) * 16 :, :] = jnp.zeros(((2 * part_chunks - chunks) * 16, lane), BF16)
    lax.fori_loop(1, micros, plan, 0)

    order = schedule(micros)

    def stage(i, _):
        kind, m = jnp.int32(order[0][0]), jnp.int32(order[0][1])
        for index, (k, micro) in enumerate(order):
            kind = jnp.where(i == index, k, kind)
            m = jnp.where(i == index, micro, m)

        @pl.when(kind == 0)
        def _():
            dispatch(m)

        @pl.when(kind == 1)
        def _():
            run_experts(m)

        @pl.when(kind == 2)
        def _():
            combine(m)

        return 0

    lax.fori_loop(0, len(order), stage, 0)

    @pl.when(section < sections - 1)
    def _():
        for q in range(2):
            pltpu.make_async_copy(finished[q], finished[q], finished_sem.at[q]).wait()

    result[0] = unfold([finished[q][...] for q in range(2)]).astype(BF16)

    @pl.when(section != 0)
    def _():
        for copy in first_copies:
            copy.wait_send()

    def drain(m, _):
        for q in range(2):
            for source, semaphore in ((dispatched, dispatch_send), (produced, produce_send)):
                view = source.at[m, q, pl.ds(0, len(partners)), pl.ds(0, sent[q])]
                pltpu.make_async_copy(view, view, semaphore.at[m, q]).wait()

        @pl.when((section < sections - 1) | (m < micros - 1))
        def _():
            for q in range(2):
                pltpu.make_async_copy(outgoing[q].at[m], outgoing[q].at[m], hidden_send.at[m, q]).wait()

        return 0

    lax.fori_loop(0, micros, drain, 0)


def solution(mesh):
    sections = mesh.shape["section"]
    experts = mesh.shape["expert"]
    grid_z = grid_x = int(round((experts // 2) ** 0.5))

    def per_device(tokens, norm_gain, router, w_gate, w_up, w_down, expert_ids):
        rows, width = tokens.shape[1:]
        inner_width = w_gate.shape[3]
        chunks = width // lane
        micros = expert_ids.shape[1]
        slots = experts * capacity
        messages = experts * part_rows
        vmem = pl.BlockSpec(memory_space=pltpu.VMEM)
        anywhere = pl.BlockSpec(memory_space=pl.ANY)
        dma = pltpu.SemaphoreType.DMA
        packed = [(2 * rows, part_chunks * lane // 2), (2 * rows, (width - part_chunks * lane) // 2)]
        return pl.pallas_call(
            functools.partial(kernel, grid_z, grid_x, sections, chunks),
            out_shape=jax.ShapeDtypeStruct(tokens.shape, BF16),
            in_specs=[vmem, vmem, vmem, anywhere, anywhere, anywhere, vmem],
            out_specs=vmem,
            scratch_shapes=[
                pltpu.VMEM((width, inner_width), BF16),
                pltpu.VMEM((width, inner_width), BF16),
                pltpu.VMEM((inner_width, width), BF16),
                pltpu.VMEM((micros,) + packed[0], BF16),
                pltpu.VMEM((micros,) + packed[1], BF16),
                pltpu.VMEM(packed[0], BF16),
                pltpu.VMEM(packed[1], BF16),
                pltpu.VMEM(packed[0], BF16),
                pltpu.VMEM(packed[1], BF16),
                pltpu.VMEM((micros,) + packed[0], BF16),
                pltpu.VMEM((micros,) + packed[1], BF16),
                pltpu.VMEM((micros, messages, lane), BF16),
                pltpu.VMEM((micros, capacity, rows, experts), F32),
                pltpu.VMEM((micros, part_chunks * 16, messages), BF16),
                pltpu.VMEM((micros, part_chunks * rows, 2 * lane), BF16),
                pltpu.VMEM((micros, 2, experts, part_rows, lane), BF16),
                pltpu.VMEM((micros, 2, experts, part_rows, lane), BF16),
                pltpu.VMEM((micros, 2, experts, part_rows, lane), BF16),
                pltpu.VMEM((micros, 2, experts, part_rows, lane), BF16),
                pltpu.VMEM((slots, width), BF16),
                pltpu.VMEM((slots, inner_width), F32),
                pltpu.VMEM((slots, inner_width), F32),
                pltpu.VMEM((slots, inner_width), BF16),
                pltpu.VMEM((2, experts // 8, part_chunks * 16, lane), BF16),
                pltpu.VMEM((8 * part_rows, 8 * part_rows), BF16),
                pltpu.VMEM((8 * part_rows, 8 * part_rows), BF16),
                pltpu.VMEM((capacity, experts, messages), BF16),
                pltpu.VMEM((part_chunks * 16, lane), BF16),
                dma, dma, dma,
                dma((micros, 2)), dma((micros, 2)), dma((2,)),
                dma((micros, 2)), dma((micros, 2)), dma((micros, 2)), dma((micros, 2)), dma((2,)),
            ],
            compiler_params=pltpu.CompilerParams(
                collective_id=0, has_side_effects=True, vmem_limit_bytes=58 * 2**20
            ),
            name="expert_layers",
        )(tokens, norm_gain, jnp.swapaxes(router, 1, 2), w_gate, w_up, w_down, expert_ids)

    placed = (
        P("section", "expert", None),
        P("section", None),
        P("section", None, None),
        P("section", "expert", None, None),
        P("section", "expert", None, None),
        P("section", "expert", None, None),
        P("section", None, "expert", None),
    )
    return jax.shard_map(
        per_device,
        mesh=mesh,
        in_specs=placed,
        out_specs=P("section", "expert", None),
        check_vma=False,
    )
```

```python
import functools

import jax
import jax.numpy as jnp
from jax import lax
from jax.experimental import pallas as pl
from jax.experimental.pallas import tpu as pltpu
from jax.sharding import PartitionSpec as P

MESH = pl.DeviceIdType.MESH
BF16 = jnp.bfloat16
F32 = jnp.float32

epsilon = 1e-06
routed_scale = 2.5
capacity = 2
lane = 128
part_chunks = 16
part_rows = part_chunks * capacity


def dot(a, b):
    return jnp.dot(a, b, preferred_element_type=F32)


def iota(shape, dim):
    return lax.broadcasted_iota(jnp.int32, shape, dim)


def ones_where(mask, dtype=BF16):
    return jnp.where(mask, 1.0, 0.0).astype(dtype)


def schedule(micros):
    order = []
    for m in range(0, micros, 2):
        if m:
            order += [(2, m - 2), (0, m), (2, m - 1), (0, m + 1), (1, m), (1, m + 1)]
        else:
            order += [(0, 0), (0, 1), (1, 0), (1, 1)]
    return order + [(2, micros - 2), (2, micros - 1)]


def kernel(
    grid_z, grid_x, sections, chunks, tokens, gain, router, w_gate, w_up, w_down, ids, result,
    gate_v, up_v, down_v, hidden_a, hidden_b, finished_a, finished_b, staged_a, staged_b, outgoing_a, outgoing_b,
    place, pick, factors, stacked, dispatched, arrived, produced, returned,
    rows_in, gate_sum, up_sum, inner, columns, select, select_t, spread, mask_j,
    gate_sem, up_sem, down_sem, hidden_sem, hidden_send, finished_sem,
    dispatch_send, arrive_sem, produce_send, return_sem, local_sem,
):
    section = lax.axis_index("section")
    me = lax.axis_index("expert")
    experts = grid_z * grid_x * 2
    micros = sections
    rows = 8
    width = chunks * lane
    inner_width = gate_v.shape[1]
    core, x, z = lax.rem(me, 2), lax.rem(me // 2, grid_x), me // (2 * grid_x)

    def distance(step, size):
        return min(step, size - step)

    offsets = [(da, db, dc) for dc in range(2) for da in range(grid_z) for db in range(grid_x)]
    offsets.sort(key=lambda o: -(distance(o[0], grid_z) + distance(o[1], grid_x)))
    partners = []
    for da, db, dc in offsets:
        if (da, db, dc) == (0, 0, 0):
            continue
        dz, dx = jnp.where(core == 0, da, db), jnp.where(core == 0, db, da)
        odd = lax.rem(x + z, 2) == 1
        dz, dx = jnp.where(odd, grid_z - dz, dz), jnp.where(odd, grid_x - dx, dx)
        partners.append(
            lax.rem(z + dz, grid_z) * (2 * grid_x) + lax.rem(x + dx, grid_x) * 2 + lax.rem(core + dc, 2)
        )

    copy_gate = pltpu.make_async_copy(w_gate.at[0, 0], gate_v, gate_sem)
    copy_up = pltpu.make_async_copy(w_up.at[0, 0], up_v, up_sem)
    copy_down = pltpu.make_async_copy(w_down.at[0, 0], down_v, down_sem)
    copy_gate.start()
    copy_up.start()
    copy_down.start()

    hidden, finished = (hidden_a, hidden_b), (finished_a, finished_b)
    staged, outgoing = (staged_a, staged_b), (outgoing_a, outgoing_b)
    parts = [(0, part_chunks), (part_chunks, chunks)]
    sent = [(last - first) * capacity for first, last in parts]

    for room in (arrived, returned):
        for m in range(micros):
            room[m, 1, :, part_rows - 16 :, :] = jnp.zeros((experts, 16, lane), BF16)

    barrier = pltpu.get_barrier_semaphore()
    for partner in partners:
        pl.semaphore_signal(barrier, inc=1, device_id={"expert": partner}, device_id_type=MESH)
    for step in range(1, sections):
        pl.semaphore_signal(
            barrier, inc=1, device_id={"section": lax.rem(section + step, sections)}, device_id_type=MESH
        )

    tail = (chunks - part_chunks) * rows
    for m in range(micros):
        stacked[m, tail:, lane:] = jnp.zeros((part_chunks * rows - tail, lane), BF16)

    shape = (part_rows, lane)
    r, c = iota(shape, 0), iota(shape, 1)
    diagonal = [
        jnp.where((c // rows == r // capacity) & (r % capacity == p), 1.0, 0.0).astype(F32)
        for p in range(capacity)
    ]
    repeat = jnp.where(iota((rows, lane), 1) % rows == iota((rows, lane), 0), 1.0, 0.0).astype(F32)
    token_of = iota((rows, experts), 0)
    expert_of = iota((rows, experts), 1)

    def plan(m, _=0):
        choices = ids[0, m]
        hit = jnp.zeros((rows, experts), F32)
        for k in range(choices.shape[1]):
            hit = hit + jnp.where(choices[:, k : k + 1] == expert_of, 1.0, 0.0)
        before = jnp.zeros((rows, experts), F32)
        for t in range(rows - 1):
            before = before + jnp.where(token_of > t, 1.0, 0.0) * hit[t : t + 1, :]
        lanes = []
        for p in range(capacity):
            taken = jnp.where(before == float(p), hit, 0.0)
            pick[m, p] = taken
            lanes.append(
                lax.dot_general(taken, repeat, (((0,), (0,)), ((), ())), preferred_element_type=F32)
            )
        for e in range(experts):
            block = diagonal[0] * lanes[0][e : e + 1, :] + diagonal[1] * lanes[1][e : e + 1, :]
            place[m, e * part_rows : (e + 1) * part_rows, :] = block.astype(BF16)
        return 0

    def fold(part):
        middle = part.shape[1] // 2
        return jnp.concatenate([part[:, :middle], part[:, middle:]], axis=0).astype(BF16)

    def unfold(refs):
        pieces = []
        for packed in refs:
            packed = packed.astype(F32)
            pieces += [packed[:rows], packed[rows:]]
        return jnp.concatenate(pieces, axis=1)

    def load_hidden(m):
        return unfold([hidden[q][m] for q in range(2)])

    def normalize(m):
        values = load_hidden(m)
        inverse_rms = lax.rsqrt(jnp.mean(values * values, axis=-1, keepdims=True) + epsilon)
        return values * inverse_rms * gain[...].astype(F32)

    def fill_slots(m):
        normed = normalize(m)
        for q, (first, last) in enumerate(parts):
            stacked[m, : (last - first) * rows, q * lane : (q + 1) * lane] = jnp.concatenate(
                [normed[:, j * lane : (j + 1) * lane] for j in range(first, last)], axis=0
            ).astype(BF16)
        slots = dot(place[m], stacked[m]).astype(BF16)
        for q in range(2):
            dispatched[m, q] = slots[:, q * lane : (q + 1) * lane].reshape(experts, part_rows, lane)

    def send(m, q, source, target, send_sem, receive_sem):
        for partner in partners:
            pltpu.make_async_remote_copy(
                src_ref=source.at[m, q, partner, pl.ds(0, sent[q])],
                dst_ref=target.at[m, q, me, pl.ds(0, sent[q])],
                send_sem=send_sem.at[m, q], recv_sem=receive_sem.at[m, q],
                device_id={"expert": partner}, device_id_type=MESH,
            ).start()
        pltpu.make_async_copy(
            source.at[m, q, me, pl.ds(0, sent[q])],
            target.at[m, q, me, pl.ds(0, sent[q])],
            receive_sem.at[m, q],
        ).start()

    def receive(m, q, target, receive_sem):
        view = target.at[m, q, :, pl.ds(0, sent[q])]
        pltpu.make_async_copy(view, view, receive_sem.at[m, q]).wait()

    def send_slots(m):
        for q in range(2):
            send(m, q, dispatched, arrived, dispatch_send, arrive_sem)

    def spread_factors(m):
        normed = normalize(m)
        twice = jnp.concatenate([normed, normed], axis=0).astype(BF16)
        logits = lax.dot_general(
            twice, router[0], (((1,), (1,)), ((), ())), preferred_element_type=F32
        )
        scores = jax.nn.sigmoid(logits[:rows])
        kept = [pick[m, p] for p in range(capacity)]
        chosen = jnp.zeros((rows, experts), F32)
        for k in range(ids.shape[3]):
            chosen = chosen + jnp.where(ids[0, m][:, k : k + 1] == expert_of, scores, 0.0)
        weights = routed_scale * scores / jnp.sum(chosen, axis=-1, keepdims=True)
        wide = None
        for p in range(capacity):
            factor = weights * kept[p]
            high = factor.astype(BF16).astype(F32)
            both = jnp.concatenate([high, factor - high], axis=0).astype(BF16)
            part = dot(both, spread[p])
            wide = part if wide is None else wide + part
        wide = wide.astype(BF16)
        for j in range(part_chunks):
            mask = mask_j[j * 16 : (j + 1) * 16, :]
            factors[m, j * 16 : (j + 1) * 16, :] = wide * jnp.concatenate(
                [mask] * (experts * part_rows // lane), axis=1
            )

    def dispatch(m):
        @pl.when((section != 0) | (m != 0))
        def _():
            for q in (1, 0):
                pltpu.make_async_copy(hidden[q].at[m], hidden[q].at[m], hidden_sem.at[m, q]).wait()
            fill_slots(m)
            send_slots(m)

        spread_factors(m)

    def sort_rows(m, q):
        first, last = parts[q]
        for pair in range(experts // 16):
            both = [
                arrived[m, q, 16 * pair + 8 * i : 16 * pair + 8 * i + 8].reshape(8 * part_rows, lane)
                for i in range(2)
            ]
            ordered = dot(select[: (last - first) * 16, :], jnp.concatenate(both, axis=1)).astype(BF16)
            for j in range(first, last):
                tile = ordered[(j - first) * 16 : (j - first + 1) * 16, :]
                cols = slice(j * lane, (j + 1) * lane)
                rows_in[pair * 32 : pair * 32 + 16, cols] = tile[:, :lane]
                rows_in[pair * 32 + 16 : pair * 32 + 32, cols] = tile[:, lane:]

    def run_experts(m):
        split = part_chunks * lane
        receive(m, 0, arrived, arrive_sem)
        sort_rows(m, 0)

        @pl.when(m == 0)
        def _():
            copy_gate.wait()
            copy_up.wait()

        for n in range(inner_width // 256):
            cols = slice(n * 256, (n + 1) * 256)
            gate_sum[:, cols] = dot(rows_in[:, :split], gate_v[:split, cols])
            up_sum[:, cols] = dot(rows_in[:, :split], up_v[:split, cols])
        receive(m, 1, arrived, arrive_sem)
        sort_rows(m, 1)
        for n in range(inner_width // 256):
            cols = slice(n * 256, (n + 1) * 256)
            gate_part = gate_sum[:, cols] + dot(rows_in[:, split:], gate_v[split:, cols])
            up_part = up_sum[:, cols] + dot(rows_in[:, split:], up_v[split:, cols])
            inner[:, cols] = (gate_part / (1.0 + jnp.exp(-gate_part)) * up_part).astype(BF16)

        @pl.when(m == 0)
        def _():
            copy_down.wait()

        step = 4
        for q, (first, last) in reversed(list(enumerate(parts))):
            for n in range(first, last, step):
                out = dot(inner[...], down_v[:, n * lane : (n + step) * lane]).astype(BF16)
                for g in range(experts // 8):
                    for j in range(step):
                        columns[q, g, (n - first + j) * 16 : (n - first + j + 1) * 16, :] = out[
                            g * 16 : (g + 1) * 16, j * lane : (j + 1) * lane
                        ]
            for pair in range(experts // 16):
                both = jnp.concatenate([columns[q, 2 * pair], columns[q, 2 * pair + 1]], axis=1)
                back = dot(select_t[...], both).astype(BF16)
                for i in range(2):
                    produced[m, q, 16 * pair + 8 * i : 16 * pair + 8 * i + 8] = back[
                        :, i * lane : (i + 1) * lane
                    ].reshape(8, part_rows, lane)
            send(m, q, produced, returned, produce_send, return_sem)

    def combine(m):
        for q in (1, 0):
            first, last = parts[q]
            receive(m, q, returned, return_sem)
            branch = dot(factors[m], returned[m, q].reshape(experts * part_rows, lane))
            values = unfold([hidden[q][m]])
            fresh = []
            for j in range(last - first):
                part = branch[j * 16 : j * 16 + 8, :] + branch[j * 16 + 8 : j * 16 + 16, :]
                fresh.append(values[:, j * lane : (j + 1) * lane] + part)
            outgoing[q][m] = fold(jnp.concatenate(fresh, axis=1))
            pass_on(m, q)

    def pass_on(m, q):
        @pl.when(section < sections - 1)
        def _():
            pltpu.make_async_remote_copy(
                src_ref=outgoing[q].at[m], dst_ref=hidden[q].at[m],
                send_sem=hidden_send.at[m, q], recv_sem=hidden_sem.at[m, q],
                device_id={"section": lax.rem(section + 1, sections)}, device_id_type=MESH,
            ).start()

        @pl.when((section == sections - 1) & (m < micros - 1))
        def _():
            pltpu.make_async_remote_copy(
                src_ref=outgoing[q].at[m], dst_ref=finished[q],
                send_sem=hidden_send.at[m, q], recv_sem=finished_sem.at[q],
                device_id={"section": lax.rem(m, sections)}, device_id_type=MESH,
            ).start()

        @pl.when((section == sections - 1) & (m == micros - 1))
        def _():
            finished[q][...] = outgoing[q][m]

    held = tokens[0].astype(F32)
    for q, (first, last) in enumerate(parts):
        staged[q][...] = fold(held[:, first * lane : last * lane])
    plan(0)

    @pl.when(section == 0)
    def _():
        for q in range(2):
            hidden[q][0] = staged[q][...]
        fill_slots(0)

    pl.semaphore_wait(barrier, len(partners) + sections - 1)

    first_copies = [
        pltpu.make_async_remote_copy(
            src_ref=staged[q], dst_ref=hidden[q].at[section],
            send_sem=local_sem.at[q], recv_sem=hidden_sem.at[section, q],
            device_id={"section": 0}, device_id_type=MESH,
        )
        for q in range(2)
    ]

    @pl.when(section == 0)
    def _():
        send_slots(0)

    @pl.when(section != 0)
    def _():
        for copy in first_copies:
            copy.start()

    shape = (8 * part_rows, 8 * part_rows)
    r, c = iota(shape, 0), iota(shape, 1)
    select[...] = ones_where(c == ((r % 16) // 2) * part_rows + (r // 16) * 2 + r % 2)
    select_t[...] = ones_where(r == ((c % 16) // 2) * part_rows + (c // 16) * 2 + c % 2)
    shape = (experts, experts * part_rows)
    r, c = iota(shape, 0), iota(shape, 1)
    for p in range(capacity):
        spread[p] = ones_where((c // part_rows == r) & (c % capacity == p))
    shape = (part_chunks * 16, lane)
    r, c = iota(shape, 0), iota(shape, 1)
    mask_j[...] = ones_where((c % part_rows) // capacity == r // 16)
    for g in range(experts // 8):
        columns[1, g, (chunks - part_chunks) * 16 :, :] = jnp.zeros(((2 * part_chunks - chunks) * 16, lane), BF16)
    lax.fori_loop(1, micros, plan, 0)

    order = schedule(micros)

    def stage(i, _):
        kind, m = jnp.int32(order[0][0]), jnp.int32(order[0][1])
        for index, (k, micro) in enumerate(order):
            kind = jnp.where(i == index, k, kind)
            m = jnp.where(i == index, micro, m)

        @pl.when(kind == 0)
        def _():
            dispatch(m)

        @pl.when(kind == 1)
        def _():
            run_experts(m)

        @pl.when(kind == 2)
        def _():
            combine(m)

        return 0

    lax.fori_loop(0, len(order), stage, 0)

    @pl.when(section < sections - 1)
    def _():
        for q in range(2):
            pltpu.make_async_copy(finished[q], finished[q], finished_sem.at[q]).wait()

    result[0] = unfold([finished[q][...] for q in range(2)]).astype(BF16)

    @pl.when(section != 0)
    def _():
        for copy in first_copies:
            copy.wait_send()

    def drain(m, _):
        for q in range(2):
            for source, semaphore in ((dispatched, dispatch_send), (produced, produce_send)):
                view = source.at[m, q, pl.ds(0, len(partners)), pl.ds(0, sent[q])]
                pltpu.make_async_copy(view, view, semaphore.at[m, q]).wait()

        @pl.when((section < sections - 1) | (m < micros - 1))
        def _():
            for q in range(2):
                pltpu.make_async_copy(outgoing[q].at[m], outgoing[q].at[m], hidden_send.at[m, q]).wait()

        return 0

    lax.fori_loop(0, micros, drain, 0)


def solution(mesh):
    sections = mesh.shape["section"]
    experts = mesh.shape["expert"]
    grid_z = grid_x = int(round((experts // 2) ** 0.5))

    def per_device(tokens, norm_gain, router, w_gate, w_up, w_down, expert_ids):
        rows, width = tokens.shape[1:]
        inner_width = w_gate.shape[3]
        chunks = width // lane
        micros = expert_ids.shape[1]
        slots = experts * capacity
        messages = experts * part_rows
        vmem = pl.BlockSpec(memory_space=pltpu.VMEM)
        anywhere = pl.BlockSpec(memory_space=pl.ANY)
        dma = pltpu.SemaphoreType.DMA
        packed = [(2 * rows, part_chunks * lane // 2), (2 * rows, (width - part_chunks * lane) // 2)]
        return pl.pallas_call(
            functools.partial(kernel, grid_z, grid_x, sections, chunks),
            out_shape=jax.ShapeDtypeStruct(tokens.shape, BF16),
            in_specs=[vmem, vmem, vmem, anywhere, anywhere, anywhere, vmem],
            out_specs=vmem,
            scratch_shapes=[
                pltpu.VMEM((width, inner_width), BF16),
                pltpu.VMEM((width, inner_width), BF16),
                pltpu.VMEM((inner_width, width), BF16),
                pltpu.VMEM((micros,) + packed[0], BF16),
                pltpu.VMEM((micros,) + packed[1], BF16),
                pltpu.VMEM(packed[0], BF16),
                pltpu.VMEM(packed[1], BF16),
                pltpu.VMEM(packed[0], BF16),
                pltpu.VMEM(packed[1], BF16),
                pltpu.VMEM((micros,) + packed[0], BF16),
                pltpu.VMEM((micros,) + packed[1], BF16),
                pltpu.VMEM((micros, messages, lane), BF16),
                pltpu.VMEM((micros, capacity, rows, experts), F32),
                pltpu.VMEM((micros, part_chunks * 16, messages), BF16),
                pltpu.VMEM((micros, part_chunks * rows, 2 * lane), BF16),
                pltpu.VMEM((micros, 2, experts, part_rows, lane), BF16),
                pltpu.VMEM((micros, 2, experts, part_rows, lane), BF16),
                pltpu.VMEM((micros, 2, experts, part_rows, lane), BF16),
                pltpu.VMEM((micros, 2, experts, part_rows, lane), BF16),
                pltpu.VMEM((slots, width), BF16),
                pltpu.VMEM((slots, inner_width), F32),
                pltpu.VMEM((slots, inner_width), F32),
                pltpu.VMEM((slots, inner_width), BF16),
                pltpu.VMEM((2, experts // 8, part_chunks * 16, lane), BF16),
                pltpu.VMEM((8 * part_rows, 8 * part_rows), BF16),
                pltpu.VMEM((8 * part_rows, 8 * part_rows), BF16),
                pltpu.VMEM((capacity, experts, messages), BF16),
                pltpu.VMEM((part_chunks * 16, lane), BF16),
                dma, dma, dma,
                dma((micros, 2)), dma((micros, 2)), dma((2,)),
                dma((micros, 2)), dma((micros, 2)), dma((micros, 2)), dma((micros, 2)), dma((2,)),
            ],
            compiler_params=pltpu.CompilerParams(
                collective_id=0, has_side_effects=True, vmem_limit_bytes=58 * 2**20
            ),
            name="expert_layers",
        )(tokens, norm_gain, jnp.swapaxes(router, 1, 2), w_gate, w_up, w_down, expert_ids)

    placed = (
        P("section", "expert", None),
        P("section", None),
        P("section", None, None),
        P("section", "expert", None, None),
        P("section", "expert", None, None),
        P("section", "expert", None, None),
        P("section", None, "expert", None),
    )
    return jax.shard_map(
        per_device,
        mesh=mesh,
        in_specs=placed,
        out_specs=P("section", "expert", None),
        check_vma=False,
    )
```
